512 devices in a mesh: shot: 64 (over x, z_hi, y, core), tm: 8 (over z_lo).
Axes of the slice: x: 4, y: 4, z: 16 (z_hi: 2, z_lo: 8; z = z_hi * 8 + z_lo), core: 2. Of those that a mesh axis runs over, the one named last changes fastest.
Arguments:
- shot_window: bfloat16 [768, 32, 256], P('shot'), may hold values from -0.125 to 0.125
- receiver_data: bfloat16 [512, 192, 256], P('tm', 'shot'), may hold values from -6 to 6
- apertures: int32 [768, 4], P('shot'), may hold values from 0 to 7
- taper_index: int32 [768, 4], P('shot'), may hold values from 0 to 15
- taper_table: float32 [16], replicated, may hold values from 0.2 to 1
Outputs:
- multiples: bfloat16 [512, 768, 192], P('tm', 'shot')
The draws below stay inside these ranges and needn't reach their ends.
All inputs are finite; a program needn't handle non-finite values.
Results may differ from the reference program's by a relative error of at most 0.012.
Values may be sent and summed in bfloat16 or wider, within the bound.
A program may use at most 128 MiB of HBM per device.

```python
import math
import jax
import jax.numpy as jnp
from jax import lax

K = 256
R = 192
NT = 512
LAG = 32
NKB = 8
APER = 4
NTAPER = 16
S = 768


def with_ends(entries, own_key, least, high):
    shape = entries.shape
    index_at = [jax.random.randint(jax.random.fold_in(own_key, axis), (), 0, shape[axis]) for axis in range(len(shape))]
    entries = entries.at[tuple(index_at)].set(least)
    longest = shape.index(max(shape))
    index_at[longest] = (index_at[longest] + 1) % shape[longest]
    return entries.at[tuple(index_at)].set(high)


def block_scale(key, extent, split, low, high):
    factor_of = 1.0
    for position, shards_of in split:
        draws = jax.random.uniform(jax.random.fold_in(jax.random.fold_in(key, 6), position), (shards_of,), jnp.float32, low / len(split), high / len(split))
        factor_of = factor_of * jnp.repeat(jnp.exp(draws), extent[position] // shards_of).reshape((-1,) + (1,) * (len(extent) - 1 - position))
    return factor_of


def scatter_about(own_key, shape, deviation, bound, shards=(), kind=jnp.bfloat16):
    gain = block_scale(own_key, shape, shards, -0.22, 0.18) if shards else 1.0
    values = jax.random.normal(own_key, shape, jnp.float32) * deviation * gain
    return jnp.minimum(jnp.maximum(values, -bound), bound).astype(kind)


def setup_inputs(seed: int = 0) -> dict:
    seeds = jax.random.split(jax.random.key(seed), 6)
    return {
        "shot_window": scatter_about(seeds[0], (S, LAG, K), (LAG * K // 4) ** -0.5, 0.125, ((0, 64),)),
        "receiver_data": scatter_about(seeds[1], (NT, R, K), 1.0, 6.0, ((0, 8), (1, 64))),
        "apertures": with_ends(jax.random.randint(seeds[2], (S, APER), 0, NKB), jax.random.fold_in(seeds[2], 1), 0, NKB - 1).astype(jnp.int32),
        "taper_index": with_ends(jax.random.randint(seeds[3], (S, APER), 0, NTAPER), jax.random.fold_in(seeds[3], 1), 0, NTAPER - 1).astype(jnp.int32),
        "taper_table": jnp.clip(jnp.exp(jax.random.uniform(seeds[4], (NTAPER,), jnp.float32, math.log(0.2), math.log(1.0))), 0.2, 1.0),
    }


def tapered_operator(shot_window, apertures, taper_index, taper_table, nblocks):
    table_size = taper_table.shape[0]
    picked = jnp.sum(jnp.where(taper_index[:, :, None] == jnp.arange(table_size, dtype=jnp.int32)[None, None, :], taper_table[None, None, :], jnp.float32(0.0)), axis=2)
    weight = jnp.sum(jnp.where(apertures[:, :, None] == jnp.arange(nblocks, dtype=jnp.int32)[None, None, :], picked[:, :, None], jnp.float32(0.0)), axis=1)
    block_size = shot_window.shape[2] // nblocks
    spread = jnp.repeat(weight, block_size, axis=1)
    return (shot_window.astype(jnp.float32) * spread[:, None, :]).astype(jnp.bfloat16)


def reference(shot_window, receiver_data, apertures, taper_index, taper_table):
    operator = tapered_operator(shot_window, apertures, taper_index, taper_table, NKB).astype(jnp.float32)
    padded = jnp.pad(receiver_data.astype(jnp.float32), ((LAG, 0), (0, 0), (0, 0)))

    def add_lag(lag, total):
        start = (LAG - lag).astype(jnp.int32)
        moved = lax.dynamic_slice_in_dim(padded, start, NT, 0)
        coef = lax.dynamic_index_in_dim(operator, lag, 1, keepdims=False)
        return total + jnp.einsum('sk,trk->tsr', coef, moved)

    total = lax.fori_loop(0, LAG, add_lag, jnp.zeros((NT, S, R), jnp.float32))
    return total.astype(jnp.bfloat16)
```

```python
import jax
import jax.numpy as jnp
from jax import lax
from jax.experimental import pallas as pl
from jax.experimental.pallas import tpu as pltpu
from jax.sharding import PartitionSpec as P

MESH = pl.DeviceIdType.MESH
NX, NY, NH, NC, NTM = 4, 4, 2, 2, 8
NZ = NH * NTM
NKB, LAG, K = 8, 32, 256
SH, RC, TS = 12, 3, 64
S2 = 2 * SH
UR = NY * RC
NCH = 3
R = 192
HEAD, ROWS, WIN = 16, 112, 96
ORDER = (0, 1, 3, 2)
HR = 80
NSEM = 80

HALF = ((0, 32), (32, 32))
PLUS = ((16, 16), (32, 16))
MINUS = ((0, 16), (48, 16))


def device(x, y, h, c, t):
    return (((x * NH + h) * NY + y) * NC + c, t)


def kernel(x_ref, shot_hbm, aper_ref, tidx_ref, table_ref, out_ref,
           xg, rz, shot_ref, op_own, op_sib, op_f32, op_all, wt, prod, main, half_f32, halo_out, halo_in,
           ex_out, ex_in, wide, send_sem, recv_sem, z_send, z_recv, op_sem, halo_sem, ex_sem, local_sem):
    shot_i = lax.axis_index("shot")
    t = lax.axis_index("tm")
    c = shot_i % 2
    y = (shot_i // 2) % 4
    h = (shot_i // 8) % 2
    x = shot_i // 16
    z = h * NTM + t
    xs = [(x + d) % NX for d in range(NX)]
    ys = [RC * ((y + d) % NY) for d in range(NY)]
    zp = (z + 4) % NZ
    zm = (z + NZ - 4) % NZ
    up = device(x, y, zp // NTM, c, zp % NTM)
    down = device(x, y, zm // NTM, c, zm % NTM)
    sibling = device(x, y, h, 1 - c, t)
    after = device(x, y, h, c, (t + 1) % NTM)
    before = device(x, y, h, c, (t + NTM - 1) % NTM)
    near = {
        ("x", 1): device((x + 1) % NX, y, h, c, t),
        ("x", -1): device((x + NX - 1) % NX, y, h, c, t),
        ("y", 1): device(x, (y + 1) % NY, h, c, t),
        ("y", -1): device(x, (y + NY - 1) % NY, h, c, t),
    }
    partners = list(near.values()) + [up, down, sibling, after, before]

    own_copy = pltpu.make_async_copy(x_ref, xg.at[0, x, pl.ds(ys[0], RC), pl.ds(HEAD, TS)], local_sem.at[0])
    own_copy.start()
    shot_copy = pltpu.make_async_copy(shot_hbm, shot_ref, local_sem.at[1])
    shot_copy.start()

    for l in range(2):
        xg[l, :, :, 0:HEAD, :] = jnp.zeros((NX, UR, HEAD, K), jnp.bfloat16)
        xg[l, :, :, HEAD + TS:ROWS, :] = jnp.zeros((NX, UR, ROWS - HEAD - TS, K), jnp.bfloat16)
    half_f32[...] = jnp.zeros_like(half_f32)

    barrier = pltpu.get_barrier_semaphore()
    for who in partners:
        pl.semaphore_signal(barrier, inc=1, device_id=who, device_id_type=MESH)
    pl.semaphore_wait(barrier, len(partners))

    sends = []
    kinds = {}

    def slot(l, dx, dy, rows):
        return xg.at[l, xs[dx % NX], pl.ds(ys[dy % NY], RC), pl.ds(HEAD + rows[0], rows[1])]

    def remote(src, dst, ssem, rsem, who):
        return pltpu.make_async_remote_copy(src_ref=src, dst_ref=dst, send_sem=ssem, recv_sem=rsem,
                                            device_id=who, device_id_type=MESH)

    def start(copy):
        copy.start()
        sends.append(copy)
        return copy

    z_first = [start(remote(x_ref.at[:, pl.ds(32 * d, 32)], rz.at[d], z_send.at[d], z_recv.at[d], who))
               for d, who in ((0, up), (1, down))]

    def send(l, n, oa, ob, rows, axis, way):
        first = "y" if n == 0 else "x"
        dx, dy = (ob, oa) if first == "y" else (oa, ob)
        step = way if axis == first else 0
        other = way if axis != first else 0
        key = (l, n, oa - step, ob - other, rows)
        k = kinds.setdefault(("sem",) + key + (axis, way), len([q for q in kinds if q[0] == "sem"]))
        ref = slot(l, dx, dy, rows)
        src = ref
        if l == 0 and oa == 0 and ob == 0:
            src = x_ref.at[:, pl.ds(rows[0], rows[1])]
        kinds[key] = start(remote(src, ref, send_sem.at[k], recv_sem.at[k], near[(axis, way)]))

    def recv(l, n, oa, ob, rows):
        kinds[(l, n, oa, ob, rows)].wait_recv()

    def axes(n):
        return ("y", "x") if n == 0 else ("x", "y")

    def base(l, n):
        a, b = axes(n)
        for axis in (a, b):
            for way in (1, -1):
                send(l, n, 0, 0, HALF[n], axis, way)

    def round1(l):
        for n in (0, 1):
            a, b = axes(n)
            for off, way, piece in ((-1, 1, PLUS), (1, -1, MINUS)):
                recv(l, n, off, 0, HALF[n])
                send(l, n, off, 0, piece[n], a, way)
                for w in (1, -1):
                    send(l, n, off, 0, HALF[n], b, w)
        for n in (0, 1):
            a, b = axes(n)
            for off, way, piece in ((-1, 1, PLUS), (1, -1, MINUS)):
                recv(l, n, 0, off, HALF[n])
                send(l, n, 0, off, piece[n], b, way)

    def round2(l):
        for n in (0, 1):
            a, b = axes(n)
            recv(l, n, -2, 0, PLUS[n])
            recv(l, n, 2, 0, MINUS[n])
            for w in (1, -1):
                send(l, n, 2, 0, HALF[n], b, w)
        for oa in (-1, 1):
            for n in (0, 1):
                a, b = axes(n)
                for off, way, piece in ((-1, 1, PLUS), (1, -1, MINUS)):
                    recv(l, n, oa, off, HALF[n])
                    send(l, n, oa, off, piece[n], b, way)
        for n in (0, 1):
            recv(l, n, 0, -2, PLUS[n])
            recv(l, n, 0, 2, MINUS[n])

    def round3(l):
        for n in (0, 1):
            a, b = axes(n)
            for off, way, piece in ((-1, 1, PLUS), (1, -1, MINUS)):
                recv(l, n, 2, off, HALF[n])
                send(l, n, 2, off, piece[n], b, way)

    def round4(l):
        for oa in (-1, 1, 2):
            for n in (0, 1):
                recv(l, n, oa, -2, PLUS[n])
                recv(l, n, oa, 2, MINUS[n])

    base(0, 0)
    base(0, 1)

    wt[...] = jnp.zeros_like(wt)
    tidx = tidx_ref[...]
    aper = aper_ref[...]
    picked = jnp.zeros(tidx.shape, jnp.float32)
    for j in range(16):
        picked = picked + jnp.where(tidx == j, table_ref[j], jnp.float32(0.0))
    for b in range(NKB):
        wt[b:b + 1, 0:SH] = jnp.sum(jnp.where(aper == b, picked, jnp.float32(0.0)), axis=0, keepdims=True)
    weight = wt[...].T
    block = lax.broadcasted_iota(jnp.int32, (16, K), 1) // (K // NKB)
    spread = jnp.zeros((16, K), jnp.float32)
    for b in range(NKB):
        spread = jnp.where(block == b, weight[0:16, b:b + 1], spread)
    shot_copy.wait()
    for s in range(SH):
        op_own[s] = (shot_ref[s].astype(jnp.float32) * spread[s:s + 1, :]).astype(jnp.bfloat16)
    op_copy = start(remote(op_own, op_sib, op_sem.at[0], op_sem.at[1], sibling))

    round1(0)
    z_second = []
    for d, who in ((0, up), (1, down)):
        z_first[d].wait_recv()
        z_second.append(start(remote(rz.at[d], slot(1, 0, 0, HALF[d]), z_send.at[2 + d], z_recv.at[2 + d], who)))

    def place(ref, s, row):
        v = ref[s].astype(jnp.float32)
        for q in range(2):
            op_f32[q, pl.ds(row, LAG, stride=S2), :] = v[:, q * 128:(q + 1) * 128]

    for s in range(SH):
        place(op_own, s, s if s < 8 else 8 + s)
    op_copy.wait_recv()
    for s in range(SH):
        place(op_sib, s, 8 + s if s < 8 else 12 + s)
    for q in range(2):
        for a in range(2):
            cols = a * K + q * 128
            op_all[:, cols:cols + 128] = op_f32[q, a * LAG * SH:(a + 1) * LAG * SH, :].astype(jnp.bfloat16)

    lane = lax.broadcasted_iota(jnp.int32, (S2, 128), 1)

    def compute(g):
        l, ux = g // 4, xs[ORDER[g % 4]]
        for r0, nr in ((0, 8), (8, 4)):
            late = xg[l, ux, r0:r0 + nr, HEAD:HEAD + WIN, :].reshape(nr * WIN, K)
            early = xg[l, ux, r0:r0 + nr, 0:WIN, :].reshape(nr * WIN, K)
            prod[:, r0 * WIN:(r0 + nr) * WIN] = lax.dot_general(
                op_all[...], jnp.concatenate([late, early], axis=1), (((1,), (1,)), ((), ())),
                preferred_element_type=jnp.float32)
        for j in range(NCH):
            acc = prod[0:S2, j * 4 * WIN:(j + 1) * 4 * WIN]
            for b in range(1, LAG // 2):
                acc = acc + pltpu.roll(prod[b * S2:(b + 1) * S2, j * 4 * WIN:(j + 1) * 4 * WIN], b, 1)
            v0, v1, v2 = acc[:, 0:128], acc[:, 128:256], acc[:, 256:384]
            index = g * NCH + j
            main[2 * index] = jnp.where(lane < 64, v0, pltpu.roll(jnp.where(lane >= 96, v0, v1), 96, 1))
            main[2 * index + 1] = jnp.where(lane < 64, pltpu.roll(v2, 96, 1), v1)
            halo = jnp.where(lane < 32, v2, jnp.where(lane < 64, v1, jnp.where(lane < 96, v0, v2)))
            half_f32[g * HR + j * S2:g * HR + (j + 1) * S2, :] = halo

    def halo_copy(g):
        return remote(halo_out.at[g], halo_in.at[g], halo_sem.at[g], halo_sem.at[8 + g], after)

    def send_halo(g):
        halo_out[g] = half_f32[g * HR:(g + 1) * HR, :].astype(jnp.bfloat16)

        @pl.when(t < NTM - 1)
        def _():
            halo_copy(g).start()

    lane8 = lax.broadcasted_iota(jnp.int32, (8, 128), 1)

    rows_of = [xs[d] * 48 for d in ORDER]

    def widen(g, j, q, first8, second8, base_s, core):
        for k in range(2):
            ry = 4 * j + ((0, 1), (3, 2))[q][k]
            row = rows_of[g % 4] + 24 * ((h + g // 4) % 2) + core * 3 + (ry // 3) * 6 + ry % 3
            mask = (lane8 < 64) if k == 0 else (lane8 >= 64)
            wide[pl.ds(base_s * R + row, 8, stride=R), :] = jnp.where(mask, second8, 0.0)
            wide[pl.ds(row, 8, stride=R), :] = jnp.where(mask, first8, 0.0)

    def exchange_copy(g):
        rows = pl.ds(g * 2 * NCH, 2 * NCH)
        return remote(ex_out.at[rows], ex_in.at[rows], ex_sem.at[g], ex_sem.at[8 + g], sibling)

    copies = {}

    def finish(g):
        @pl.when(t > 0)
        def _():
            halo_copy(g).wait_recv()
            half_f32[g * HR:(g + 1) * HR, :] = halo_in[g].astype(jnp.float32)

        @pl.when(t == 0)
        def _():
            half_f32[g * HR:(g + 1) * HR, :] = jnp.zeros((HR, 128), jnp.float32)

        for j in range(NCH):
            packed = half_f32[g * HR + j * S2:g * HR + (j + 1) * S2, :]
            by32, by64 = pltpu.roll(packed, 32, 1), pltpu.roll(packed, 64, 1)
            for q in range(2):
                index = 2 * (g * NCH + j) + q
                part = jnp.where(lane < 64, by64, by32) if q == 0 else jnp.where(lane < 64, by32, by64)
                v = main[index] + jnp.where(lane % 64 < 32, part, 0.0)
                v = v.astype(jnp.bfloat16).astype(jnp.float32)
                ex_out[index] = v[8:24].astype(jnp.bfloat16)
                widen(g, j, q, v[0:8], v[16:24], 8, c)
        copies[g] = start(exchange_copy(g))

    def accept(g):
        copies[g].wait_recv()
        for j in range(NCH):
            for q in range(2):
                v = ex_in[2 * (g * NCH + j) + q].astype(jnp.float32)
                widen(g, j, q, v[0:8], v[8:16], 4, 1 - c)

    def unit(g):
        compute(g)
        send_halo(g)

    round2(0)
    own_copy.wait()
    unit(0)
    round3(0)
    for n in (0, 1):
        z_second[n].wait_recv()
        base(1, n)
    round4(0)
    unit(1)
    unit(2)
    round1(1)
    unit(3)
    finish(0)
    finish(1)
    round2(1)
    unit(4)
    finish(2)
    round3(1)
    finish(3)
    accept(0)
    accept(1)
    round4(1)
    unit(5)
    unit(6)
    unit(7)
    accept(2)
    accept(3)
    for g in (4, 5, 6, 7):
        finish(g)
    for g in (4, 5, 6, 7):
        accept(g)

    both = lax.broadcasted_iota(jnp.int32, (TS, 128), 1) % TS == lax.broadcasted_iota(jnp.int32, (TS, 128), 0)
    both = jnp.where(both, 1.0, 0.0).astype(jnp.bfloat16)

    def turn(s, carry):
        block = wide[pl.ds(pl.multiple_of(s * R, 8), R), :].astype(jnp.bfloat16)
        out_ref[s] = lax.dot_general(both, block, (((1,), (1,)), ((), ())),
                                     preferred_element_type=jnp.float32).astype(jnp.bfloat16)
        return carry

    lax.fori_loop(0, SH, turn, 0)

    for copy in sends:
        copy.wait_send()

    @pl.when(t < NTM - 1)
    def _():
        for g in range(8):
            halo_copy(g).wait_send()


def body(shot_window, receiver_data, apertures, taper_index, taper_table):
    gathered = jnp.transpose(receiver_data, (1, 0, 2))
    vmem = pl.BlockSpec(memory_space=pltpu.VMEM)
    bf, f4 = jnp.bfloat16, jnp.float32
    dma = pltpu.SemaphoreType.DMA
    out = pl.pallas_call(
        kernel,
        out_shape=jax.ShapeDtypeStruct((SH, TS, R), bf),
        in_specs=[pl.BlockSpec(memory_space=pl.ANY), pl.BlockSpec(memory_space=pl.ANY), vmem, vmem, pl.BlockSpec(memory_space=pltpu.SMEM)],
        out_specs=vmem,
        scratch_shapes=[
            pltpu.VMEM((2, NX, UR, ROWS, K), bf),
            pltpu.VMEM((2, RC, 32, K), bf),
            pltpu.VMEM((SH, LAG, K), bf),
            pltpu.VMEM((SH, LAG, K), bf),
            pltpu.VMEM((SH, LAG, K), bf),
            pltpu.VMEM((2, LAG * S2, 128), f4),
            pltpu.VMEM((LAG * SH, 2 * K), bf),
            pltpu.VMEM((NKB, 128), f4),
            pltpu.VMEM((LAG * SH, UR * WIN), f4),
            pltpu.VMEM((48, S2, 128), f4),
            pltpu.VMEM((8 * HR, 128), f4),
            pltpu.VMEM((8, HR, 128), bf),
            pltpu.VMEM((8, HR, 128), bf),
            pltpu.VMEM((48, 16, 128), bf),
            pltpu.VMEM((48, 16, 128), bf),
            pltpu.VMEM((16 * R, 128), f4),
            dma((NSEM,)), dma((NSEM,)), dma((4,)), dma((4,)), dma((2,)), dma((16,)), dma((16,)), dma((2,)),
        ],
        compiler_params=pltpu.CompilerParams(collective_id=0, has_side_effects=True,
                                             vmem_limit_bytes=60 * 1024 * 1024),
    )(gathered, shot_window, apertures.T, taper_index.T, taper_table)
    return jnp.transpose(out, (1, 0, 2))


def solution(mesh):
    in_specs = (P("shot", None, None), P("tm", "shot", None), P("shot", None), P("shot", None), P())
    out_specs = P("tm", "shot", None)
    return jax.shard_map(body, mesh=mesh, in_specs=in_specs, out_specs=out_specs, check_vma=False)
```

```python
import jax
import jax.numpy as jnp
from jax import lax
from jax.experimental import pallas as pl
from jax.experimental.pallas import tpu as pltpu
from jax.sharding import PartitionSpec as P

MESH = pl.DeviceIdType.MESH
NX, NY, NH, NC, NTM = 4, 4, 2, 2, 8
NZ = NH * NTM
NKB, LAG, K = 8, 32, 256
SH, RC, TS = 12, 3, 64
S2 = 2 * SH
UR = NY * RC
NCH = 3
R = 192
HEAD, ROWS, WIN = 16, 112, 96
ORDER = (0, 1, 3, 2)
HR = 80
NSEM = 80

HALF = ((0, 32), (32, 32))
PLUS = ((16, 16), (32, 16))
MINUS = ((0, 16), (48, 16))


def device(x, y, h, c, t):
    return (((x * NH + h) * NY + y) * NC + c, t)


def kernel(x_ref, shot_hbm, aper_hbm, tidx_hbm, table_hbm, out_ref,
           xg, rz, aper_ref, tidx_ref, table_ref, shot_ref, op_own, op_sib, op_f32, op_all, wt, prod, main, half_f32, halo_out, halo_in,
           ex_out, ex_in, wide, send_sem, recv_sem, z_send, z_recv, op_sem, halo_sem, ex_sem, local_sem):
    shot_i = lax.axis_index("shot")
    t = lax.axis_index("tm")
    c = shot_i % 2
    y = (shot_i // 2) % 4
    h = (shot_i // 8) % 2
    x = shot_i // 16
    z = h * NTM + t
    xs = [(x + d) % NX for d in range(NX)]
    ys = [RC * ((y + d) % NY) for d in range(NY)]
    zp = (z + 4) % NZ
    zm = (z + NZ - 4) % NZ
    up = device(x, y, zp // NTM, c, zp % NTM)
    down = device(x, y, zm // NTM, c, zm % NTM)
    sibling = device(x, y, h, 1 - c, t)
    after = device(x, y, h, c, (t + 1) % NTM)
    before = device(x, y, h, c, (t + NTM - 1) % NTM)
    near = {
        ("x", 1): device((x + 1) % NX, y, h, c, t),
        ("x", -1): device((x + NX - 1) % NX, y, h, c, t),
        ("y", 1): device(x, (y + 1) % NY, h, c, t),
        ("y", -1): device(x, (y + NY - 1) % NY, h, c, t),
    }
    partners = list(near.values()) + [up, down, sibling, after, before]

    barrier = pltpu.get_barrier_semaphore()
    for who in partners:
        pl.semaphore_signal(barrier, inc=1, device_id=who, device_id_type=MESH)
    own_copy = pltpu.make_async_copy(x_ref, xg.at[0, x, pl.ds(ys[0], RC), pl.ds(HEAD, TS)], local_sem.at[0])
    own_copy.start()
    shot_copy = pltpu.make_async_copy(shot_hbm, shot_ref, local_sem.at[1])
    shot_copy.start()
    small = [pltpu.make_async_copy(a, b, local_sem.at[2 + i])
             for i, (a, b) in enumerate(((aper_hbm, aper_ref), (tidx_hbm, tidx_ref), (table_hbm, table_ref)))]
    for copy in small:
        copy.start()

    pl.semaphore_wait(barrier, len(partners))

    sends = []
    kinds = {}

    def slot(l, dx, dy, rows):
        return xg.at[l, xs[dx % NX], pl.ds(ys[dy % NY], RC), pl.ds(HEAD + rows[0], rows[1])]

    def remote(src, dst, ssem, rsem, who):
        return pltpu.make_async_remote_copy(src_ref=src, dst_ref=dst, send_sem=ssem, recv_sem=rsem,
                                            device_id=who, device_id_type=MESH)

    def start(copy):
        copy.start()
        sends.append(copy)
        return copy

    z_first = [start(remote(x_ref.at[:, pl.ds(32 * d, 32)], rz.at[d], z_send.at[d], z_recv.at[d], who))
               for d, who in ((0, up), (1, down))]

    def send(l, n, oa, ob, rows, axis, way):
        first = "y" if n == 0 else "x"
        dx, dy = (ob, oa) if first == "y" else (oa, ob)
        step = way if axis == first else 0
        other = way if axis != first else 0
        key = (l, n, oa - step, ob - other, rows)
        k = kinds.setdefault(("sem",) + key + (axis, way), len([q for q in kinds if q[0] == "sem"]))
        ref = slot(l, dx, dy, rows)
        src = ref
        if l == 0 and oa == 0 and ob == 0:
            src = x_ref.at[:, pl.ds(rows[0], rows[1])]
        kinds[key] = start(remote(src, ref, send_sem.at[k], recv_sem.at[k], near[(axis, way)]))

    def recv(l, n, oa, ob, rows):
        kinds[(l, n, oa, ob, rows)].wait_recv()

    def axes(n):
        return ("y", "x") if n == 0 else ("x", "y")

    def base(l, n):
        a, b = axes(n)
        for axis in (a, b):
            for way in (1, -1):
                send(l, n, 0, 0, HALF[n], axis, way)

    def round1(l):
        for n in (0, 1):
            a, b = axes(n)
            for off, way, piece in ((-1, 1, PLUS), (1, -1, MINUS)):
                recv(l, n, off, 0, HALF[n])
                send(l, n, off, 0, piece[n], a, way)
                for w in (1, -1):
                    send(l, n, off, 0, HALF[n], b, w)
        for n in (0, 1):
            a, b = axes(n)
            for off, way, piece in ((-1, 1, PLUS), (1, -1, MINUS)):
                recv(l, n, 0, off, HALF[n])
                send(l, n, 0, off, piece[n], b, way)

    def round2(l):
        for n in (0, 1):
            a, b = axes(n)
            recv(l, n, -2, 0, PLUS[n])
            recv(l, n, 2, 0, MINUS[n])
            for w in (1, -1):
                send(l, n, 2, 0, HALF[n], b, w)
        for oa in (-1, 1):
            for n in (0, 1):
                a, b = axes(n)
                for off, way, piece in ((-1, 1, PLUS), (1, -1, MINUS)):
                    recv(l, n, oa, off, HALF[n])
                    send(l, n, oa, off, piece[n], b, way)
        for n in (0, 1):
            recv(l, n, 0, -2, PLUS[n])
            recv(l, n, 0, 2, MINUS[n])

    def round3(l):
        for n in (0, 1):
            a, b = axes(n)
            for off, way, piece in ((-1, 1, PLUS), (1, -1, MINUS)):
                recv(l, n, 2, off, HALF[n])
                send(l, n, 2, off, piece[n], b, way)

    def last(l, n, oa):
        recv(l, n, oa, -2, PLUS[n])
        recv(l, n, oa, 2, MINUS[n])

    def round4(l):
        for oa in (-1, 1, 2):
            for n in (0, 1):
                last(l, n, oa)

    base(0, 0)
    base(0, 1)

    for l in range(2):
        xg[l, :, :, 0:HEAD, :] = jnp.zeros((NX, UR, HEAD, K), jnp.bfloat16)
        xg[l, :, :, HEAD + TS:ROWS, :] = jnp.zeros((NX, UR, ROWS - HEAD - TS, K), jnp.bfloat16)
    half_f32[...] = jnp.zeros_like(half_f32)

    for copy in small:
        copy.wait()
    wt[...] = jnp.zeros_like(wt)
    tidx = tidx_ref[...]
    aper = aper_ref[...]
    picked = jnp.zeros(tidx.shape, jnp.float32)
    for j in range(16):
        picked = picked + jnp.where(tidx == j, table_ref[j], jnp.float32(0.0))
    for b in range(NKB):
        wt[b:b + 1, 0:SH] = jnp.sum(jnp.where(aper == b, picked, jnp.float32(0.0)), axis=0, keepdims=True)
    weight = wt[...].T
    block = lax.broadcasted_iota(jnp.int32, (16, K), 1) // (K // NKB)
    spread = jnp.zeros((16, K), jnp.float32)
    for b in range(NKB):
        spread = jnp.where(block == b, weight[0:16, b:b + 1], spread)
    shot_copy.wait()
    for s in range(SH):
        op_own[s] = (shot_ref[s].astype(jnp.float32) * spread[s:s + 1, :]).astype(jnp.bfloat16)
    op_copy = start(remote(op_own, op_sib, op_sem.at[0], op_sem.at[1], sibling))

    round1(0)
    z_second = []
    for d, who in ((0, up), (1, down)):
        z_first[d].wait_recv()
        z_second.append(start(remote(rz.at[d], slot(1, 0, 0, HALF[d]), z_send.at[2 + d], z_recv.at[2 + d], who)))

    def place(ref, s, row):
        v = ref[s].astype(jnp.float32)
        for q in range(2):
            op_f32[q, pl.ds(row, LAG, stride=S2), :] = v[:, q * 128:(q + 1) * 128]

    for s in range(SH):
        place(op_own, s, s if s < 8 else 8 + s)
    op_copy.wait_recv()
    for s in range(SH):
        place(op_sib, s, 8 + s if s < 8 else 12 + s)
    for q in range(2):
        for a in range(2):
            cols = a * K + q * 128
            op_all[:, cols:cols + 128] = op_f32[q, a * LAG * SH:(a + 1) * LAG * SH, :].astype(jnp.bfloat16)

    lane = lax.broadcasted_iota(jnp.int32, (S2, 128), 1)

    def compute(g):
        l, ux = g // 4, xs[ORDER[g % 4]]
        for r0, nr in ((0, 8), (8, 4)):
            late = xg[l, ux, r0:r0 + nr, HEAD:HEAD + WIN, :].reshape(nr * WIN, K)
            early = xg[l, ux, r0:r0 + nr, 0:WIN, :].reshape(nr * WIN, K)
            prod[:, r0 * WIN:(r0 + nr) * WIN] = lax.dot_general(
                op_all[...], jnp.concatenate([late, early], axis=1), (((1,), (1,)), ((), ())),
                preferred_element_type=jnp.float32)
        for j in range(NCH):
            acc = prod[0:S2, j * 4 * WIN:(j + 1) * 4 * WIN]
            for b in range(1, LAG // 2):
                acc = acc + pltpu.roll(prod[b * S2:(b + 1) * S2, j * 4 * WIN:(j + 1) * 4 * WIN], b, 1)
            v0, v1, v2 = acc[:, 0:128], acc[:, 128:256], acc[:, 256:384]
            index = g * NCH + j
            main[2 * index] = jnp.where(lane < 64, v0, pltpu.roll(jnp.where(lane >= 96, v0, v1), 96, 1))
            main[2 * index + 1] = jnp.where(lane < 64, pltpu.roll(v2, 96, 1), v1)
            halo = jnp.where(lane < 32, v2, jnp.where(lane < 64, v1, jnp.where(lane < 96, v0, v2)))
            half_f32[g * HR + j * S2:g * HR + (j + 1) * S2, :] = halo

    def halo_copy(g):
        return remote(halo_out.at[g], halo_in.at[g], halo_sem.at[g], halo_sem.at[8 + g], after)

    def send_halo(g):
        halo_out[g] = half_f32[g * HR:(g + 1) * HR, :].astype(jnp.bfloat16)

        @pl.when(t < NTM - 1)
        def _():
            halo_copy(g).start()

    lane8 = lax.broadcasted_iota(jnp.int32, (8, 128), 1)

    rows_of = [xs[d] * 48 for d in ORDER]

    def widen(g, j, q, first8, second8, base_s, core):
        for k in range(2):
            ry = 4 * j + ((0, 1), (3, 2))[q][k]
            row = rows_of[g % 4] + 24 * ((h + g // 4) % 2) + core * 3 + (ry // 3) * 6 + ry % 3
            mask = (lane8 < 64) if k == 0 else (lane8 >= 64)
            wide[pl.ds(base_s * R + row, 8, stride=R), :] = jnp.where(mask, second8, 0.0)
            wide[pl.ds(row, 8, stride=R), :] = jnp.where(mask, first8, 0.0)

    def exchange_copy(g):
        rows = pl.ds(g * 2 * NCH, 2 * NCH)
        return remote(ex_out.at[rows], ex_in.at[rows], ex_sem.at[g], ex_sem.at[8 + g], sibling)

    copies = {}

    def finish(g):
        @pl.when(t > 0)
        def _():
            halo_copy(g).wait_recv()
            half_f32[g * HR:(g + 1) * HR, :] = halo_in[g].astype(jnp.float32)

        @pl.when(t == 0)
        def _():
            half_f32[g * HR:(g + 1) * HR, :] = jnp.zeros((HR, 128), jnp.float32)

        for j in range(NCH):
            packed = half_f32[g * HR + j * S2:g * HR + (j + 1) * S2, :]
            by32, by64 = pltpu.roll(packed, 32, 1), pltpu.roll(packed, 64, 1)
            for q in range(2):
                index = 2 * (g * NCH + j) + q
                part = jnp.where(lane < 64, by64, by32) if q == 0 else jnp.where(lane < 64, by32, by64)
                v = main[index] + jnp.where(lane % 64 < 32, part, 0.0)
                v = v.astype(jnp.bfloat16).astype(jnp.float32)
                ex_out[index] = v[8:24].astype(jnp.bfloat16)
                widen(g, j, q, v[0:8], v[16:24], 8, c)
        copies[g] = start(exchange_copy(g))

    def accept(g):
        copies[g].wait_recv()
        for j in range(NCH):
            for q in range(2):
                v = ex_in[2 * (g * NCH + j) + q].astype(jnp.float32)
                widen(g, j, q, v[0:8], v[8:16], 4, 1 - c)

    def unit(g):
        compute(g)
        send_halo(g)

    round2(0)
    own_copy.wait()
    unit(0)
    round3(0)
    for n in (0, 1):
        z_second[n].wait_recv()
        base(1, n)
    round4(0)
    unit(1)
    unit(2)
    round1(1)
    unit(3)
    finish(0)
    finish(1)
    round2(1)
    unit(4)
    finish(2)
    round3(1)
    finish(3)
    for g in range(4):
        accept(g)
    last(1, 1, 1)
    unit(5)
    last(1, 1, -1)
    unit(6)
    last(1, 1, 2)
    for oa in (-1, 1, 2):
        last(1, 0, oa)
    unit(7)
    for g in (4, 5, 6, 7):
        finish(g)
    for g in (4, 5, 6, 7):
        accept(g)

    both = lax.broadcasted_iota(jnp.int32, (TS, 128), 1) % TS == lax.broadcasted_iota(jnp.int32, (TS, 128), 0)
    both = jnp.where(both, 1.0, 0.0).astype(jnp.bfloat16)

    def turn(s, carry):
        block = wide[pl.ds(pl.multiple_of(s * R, 8), R), :].astype(jnp.bfloat16)
        out_ref[s] = lax.dot_general(both, block, (((1,), (1,)), ((), ())),
                                     preferred_element_type=jnp.float32).astype(jnp.bfloat16)
        return carry

    lax.fori_loop(0, SH, turn, 0)

    for copy in sends:
        copy.wait_send()

    @pl.when(t < NTM - 1)
    def _():
        for g in range(8):
            halo_copy(g).wait_send()


def body(shot_window, receiver_data, apertures, taper_index, taper_table):
    gathered = jnp.transpose(receiver_data, (1, 0, 2))
    vmem = pl.BlockSpec(memory_space=pltpu.VMEM)
    bf, f4 = jnp.bfloat16, jnp.float32
    dma = pltpu.SemaphoreType.DMA
    out = pl.pallas_call(
        kernel,
        out_shape=jax.ShapeDtypeStruct((SH, TS, R), bf),
        in_specs=[pl.BlockSpec(memory_space=pltpu.HBM)] * 5,
        out_specs=vmem,
        scratch_shapes=[
            pltpu.VMEM((2, NX, UR, ROWS, K), bf),
            pltpu.VMEM((2, RC, 32, K), bf),
            pltpu.VMEM((4, SH), jnp.int32),
            pltpu.VMEM((4, SH), jnp.int32),
            pltpu.SMEM((16,), f4),
            pltpu.VMEM((SH, LAG, K), bf),
            pltpu.VMEM((SH, LAG, K), bf),
            pltpu.VMEM((SH, LAG, K), bf),
            pltpu.VMEM((2, LAG * S2, 128), f4),
            pltpu.VMEM((LAG * SH, 2 * K), bf),
            pltpu.VMEM((NKB, 128), f4),
            pltpu.VMEM((LAG * SH, UR * WIN), f4),
            pltpu.VMEM((48, S2, 128), f4),
            pltpu.VMEM((8 * HR, 128), f4),
            pltpu.VMEM((8, HR, 128), bf),
            pltpu.VMEM((8, HR, 128), bf),
            pltpu.VMEM((48, 16, 128), bf),
            pltpu.VMEM((48, 16, 128), bf),
            pltpu.VMEM((16 * R, 128), f4),
            dma((NSEM,)), dma((NSEM,)), dma((4,)), dma((4,)), dma((2,)), dma((16,)), dma((16,)), dma((5,)),
        ],
        compiler_params=pltpu.CompilerParams(collective_id=0, has_side_effects=True,
                                             vmem_limit_bytes=60 * 1024 * 1024),
    )(gathered, shot_window, apertures.T, taper_index.T, taper_table)
    return jnp.transpose(out, (1, 0, 2))


def solution(mesh):
    in_specs = (P("shot", None, None), P("tm", "shot", None), P("shot", None), P("shot", None), P())
    out_specs = P("tm", "shot", None)
    return jax.shard_map(body, mesh=mesh, in_specs=in_specs, out_specs=out_specs, check_vma=False)
```

```python
import jax
import jax.numpy as jnp
from jax import lax
from jax.experimental import pallas as pl
from jax.experimental.pallas import tpu as pltpu
from jax.sharding import PartitionSpec as P

MESH = pl.DeviceIdType.MESH
NX, NY, NH, NC, NTM = 4, 4, 2, 2, 8
NZ = NH * NTM
NKB, LAG, K = 8, 32, 256
SH, RC, TS = 12, 3, 64
S2 = 2 * SH
UR = NY * RC
NCH = 3
R = 192
STEP = 200
HEAD, ROWS, WIN = 16, 112, 96
ORDER = (0, 1, 3, 2)
HR = 80
NSEM = 80

HALF = ((0, 32), (32, 32))
PLUS = ((16, 16), (32, 16))
MINUS = ((0, 16), (48, 16))


def device(x, y, h, c, t):
    return (((x * NH + h) * NY + y) * NC + c, t)


def kernel(x_ref, shot_hbm, aper_hbm, tidx_hbm, table_hbm, out_ref,
           xg, rz, aper_ref, tidx_ref, table_ref, shot_ref, op_own, op_sib, op_f32, op_all, wt, prod, main, half_f32, halo_out, halo_in,
           ex_out, ex_in, wide, send_sem, recv_sem, z_send, z_recv, op_sem, halo_sem, ex_sem, local_sem):
    shot_i = lax.axis_index("shot")
    t = lax.axis_index("tm")
    c = shot_i % 2
    y = (shot_i // 2) % 4
    h = (shot_i // 8) % 2
    x = shot_i // 16
    z = h * NTM + t
    xs = [(x + d) % NX for d in range(NX)]
    ys = [RC * ((y + d) % NY) for d in range(NY)]
    zp = (z + 4) % NZ
    zm = (z + NZ - 4) % NZ
    up = device(x, y, zp // NTM, c, zp % NTM)
    down = device(x, y, zm // NTM, c, zm % NTM)
    sibling = device(x, y, h, 1 - c, t)
    after = device(x, y, h, c, (t + 1) % NTM)
    before = device(x, y, h, c, (t + NTM - 1) % NTM)
    near = {
        ("x", 1): device((x + 1) % NX, y, h, c, t),
        ("x", -1): device((x + NX - 1) % NX, y, h, c, t),
        ("y", 1): device(x, (y + 1) % NY, h, c, t),
        ("y", -1): device(x, (y + NY - 1) % NY, h, c, t),
    }
    partners = list(near.values()) + [up, down, sibling, after, before]

    barrier = pltpu.get_barrier_semaphore()
    for who in partners:
        pl.semaphore_signal(barrier, inc=1, device_id=who, device_id_type=MESH)
    own_copy = pltpu.make_async_copy(x_ref, xg.at[0, x, pl.ds(ys[0], RC), pl.ds(HEAD, TS)], local_sem.at[0])
    own_copy.start()
    shot_copy = pltpu.make_async_copy(shot_hbm, shot_ref, local_sem.at[1])
    shot_copy.start()
    small = [pltpu.make_async_copy(a, b, local_sem.at[2 + i])
             for i, (a, b) in enumerate(((aper_hbm, aper_ref), (tidx_hbm, tidx_ref), (table_hbm, table_ref)))]
    for copy in small:
        copy.start()

    pl.semaphore_wait(barrier, len(partners))

    sends = []
    kinds = {}

    def slot(l, dx, dy, rows):
        return xg.at[l, xs[dx % NX], pl.ds(ys[dy % NY], RC), pl.ds(HEAD + rows[0], rows[1])]

    def remote(src, dst, ssem, rsem, who):
        return pltpu.make_async_remote_copy(src_ref=src, dst_ref=dst, send_sem=ssem, recv_sem=rsem,
                                            device_id=who, device_id_type=MESH)

    def start(copy):
        copy.start()
        sends.append(copy)
        return copy

    z_first = [[start(remote(x_ref.at[pl.ds(i, 1), pl.ds(32 * d, 32)], rz.at[d, pl.ds(i, 1)],
                             z_send.at[2 * i + d], z_recv.at[2 * i + d], who))
                for d, who in ((0, up), (1, down))] for i in range(RC)]

    def send(l, n, oa, ob, rows, axis, way):
        first = "y" if n == 0 else "x"
        dx, dy = (ob, oa) if first == "y" else (oa, ob)
        step = way if axis == first else 0
        other = way if axis != first else 0
        key = (l, n, oa - step, ob - other, rows)
        k = kinds.setdefault(("sem",) + key + (axis, way), len([q for q in kinds if q[0] == "sem"]))
        ref = slot(l, dx, dy, rows)
        src = ref
        if l == 0 and oa == 0 and ob == 0:
            src = x_ref.at[:, pl.ds(rows[0], rows[1])]
        kinds[key] = start(remote(src, ref, send_sem.at[k], recv_sem.at[k], near[(axis, way)]))

    def recv(l, n, oa, ob, rows):
        kinds[(l, n, oa, ob, rows)].wait_recv()

    def axes(n):
        return ("y", "x") if n == 0 else ("x", "y")

    def base(l, n):
        a, b = axes(n)
        for axis in (a, b):
            for way in (1, -1):
                send(l, n, 0, 0, HALF[n], axis, way)

    def round1(l):
        for n in (0, 1):
            a, b = axes(n)
            for off, way, piece in ((-1, 1, PLUS), (1, -1, MINUS)):
                recv(l, n, off, 0, HALF[n])
                send(l, n, off, 0, piece[n], a, way)
                for w in (1, -1):
                    send(l, n, off, 0, HALF[n], b, w)
        for n in (0, 1):
            a, b = axes(n)
            for off, way, piece in ((-1, 1, PLUS), (1, -1, MINUS)):
                recv(l, n, 0, off, HALF[n])
                send(l, n, 0, off, piece[n], b, way)

    def round2(l):
        for n in (0, 1):
            a, b = axes(n)
            recv(l, n, -2, 0, PLUS[n])
            recv(l, n, 2, 0, MINUS[n])
            for w in (1, -1):
                send(l, n, 2, 0, HALF[n], b, w)
        for oa in (-1, 1):
            for n in (0, 1):
                a, b = axes(n)
                for off, way, piece in ((-1, 1, PLUS), (1, -1, MINUS)):
                    recv(l, n, oa, off, HALF[n])
                    send(l, n, oa, off, piece[n], b, way)
        for n in (0, 1):
            recv(l, n, 0, -2, PLUS[n])
            recv(l, n, 0, 2, MINUS[n])

    def round3(l):
        for n in (0, 1):
            a, b = axes(n)
            for off, way, piece in ((-1, 1, PLUS), (1, -1, MINUS)):
                recv(l, n, 2, off, HALF[n])
                send(l, n, 2, off, piece[n], b, way)

    def last(l, n, oa):
        recv(l, n, oa, -2, PLUS[n])
        recv(l, n, oa, 2, MINUS[n])

    def round4(l):
        for oa in (-1, 1, 2):
            for n in (0, 1):
                last(l, n, oa)

    base(0, 0)
    base(0, 1)

    for l in range(2):
        xg[l, :, :, 0:HEAD, :] = jnp.zeros((NX, UR, HEAD, K), jnp.bfloat16)
        xg[l, :, :, HEAD + TS:ROWS, :] = jnp.zeros((NX, UR, ROWS - HEAD - TS, K), jnp.bfloat16)
    half_f32[...] = jnp.zeros_like(half_f32)

    for copy in small:
        copy.wait()
    wt[...] = jnp.zeros_like(wt)
    tidx = tidx_ref[...]
    aper = aper_ref[...]
    picked = jnp.zeros(tidx.shape, jnp.float32)
    for j in range(16):
        picked = picked + jnp.where(tidx == j, table_ref[j], jnp.float32(0.0))
    for b in range(NKB):
        wt[b:b + 1, 0:SH] = jnp.sum(jnp.where(aper == b, picked, jnp.float32(0.0)), axis=0, keepdims=True)
    weight = wt[...].T
    block = lax.broadcasted_iota(jnp.int32, (16, K), 1) // (K // NKB)
    spread = jnp.zeros((16, K), jnp.float32)
    for b in range(NKB):
        spread = jnp.where(block == b, weight[0:16, b:b + 1], spread)
    shot_copy.wait()
    for s in range(SH):
        op_own[s] = (shot_ref[s].astype(jnp.float32) * spread[s:s + 1, :]).astype(jnp.bfloat16)
    op_copy = start(remote(op_own, op_sib, op_sem.at[0], op_sem.at[1], sibling))

    round1(0)
    z_second = []
    for i in range(RC):
        for d, who in ((0, up), (1, down)):
            z_first[i][d].wait_recv()
            dst = xg.at[1, x, pl.ds(ys[0] + i, 1), pl.ds(HEAD + HALF[d][0], 32)]
            k = 2 * (RC + i) + d
            z_second.append(start(remote(rz.at[d, pl.ds(i, 1)], dst, z_send.at[k], z_recv.at[k], who)))

    def place(ref, s, row):
        v = ref[s].astype(jnp.float32)
        for q in range(2):
            op_f32[q, pl.ds(row, LAG, stride=S2), :] = v[:, q * 128:(q + 1) * 128]

    for s in range(SH):
        place(op_own, s, s if s < 8 else 8 + s)
    op_copy.wait_recv()
    for s in range(SH):
        place(op_sib, s, 8 + s if s < 8 else 12 + s)
    for q in range(2):
        for a in range(2):
            cols = a * K + q * 128
            op_all[:, cols:cols + 128] = op_f32[q, a * LAG * SH:(a + 1) * LAG * SH, :].astype(jnp.bfloat16)

    lane = lax.broadcasted_iota(jnp.int32, (S2, 128), 1)

    def compute(g):
        l, ux = g // 4, xs[ORDER[g % 4]]
        for r0, nr in ((0, 8), (8, 4)):
            late = xg[l, ux, r0:r0 + nr, HEAD:HEAD + WIN, :].reshape(nr * WIN, K)
            early = xg[l, ux, r0:r0 + nr, 0:WIN, :].reshape(nr * WIN, K)
            prod[:, r0 * WIN:(r0 + nr) * WIN] = lax.dot_general(
                op_all[...], jnp.concatenate([late, early], axis=1), (((1,), (1,)), ((), ())),
                preferred_element_type=jnp.float32)
        for j in range(NCH):
            acc = prod[0:S2, j * 4 * WIN:(j + 1) * 4 * WIN]
            for b in range(1, LAG // 2):
                acc = acc + pltpu.roll(prod[b * S2:(b + 1) * S2, j * 4 * WIN:(j + 1) * 4 * WIN], b, 1)
            v0, v1, v2 = acc[:, 0:128], acc[:, 128:256], acc[:, 256:384]
            index = g * NCH + j
            main[2 * index] = jnp.where(lane < 64, v0, pltpu.roll(jnp.where(lane >= 96, v0, v1), 96, 1))
            main[2 * index + 1] = jnp.where(lane < 64, pltpu.roll(v2, 96, 1), v1)
            halo = jnp.where(lane < 32, v2, jnp.where(lane < 64, v1, jnp.where(lane < 96, v0, v2)))
            half_f32[g * HR + j * S2:g * HR + (j + 1) * S2, :] = halo

    def halo_copy(g):
        return remote(halo_out.at[g], halo_in.at[g], halo_sem.at[g], halo_sem.at[8 + g], after)

    def send_halo(g):
        halo_out[g] = half_f32[g * HR:(g + 1) * HR, :].astype(jnp.bfloat16)

        @pl.when(t < NTM - 1)
        def _():
            halo_copy(g).start()

    lane8 = lax.broadcasted_iota(jnp.int32, (8, 128), 1)

    rows_of = [xs[d] * 48 for d in ORDER]

    def widen(g, j, q, first8, second8, base_s, core):
        for k in range(2):
            ry = 4 * j + ((0, 1), (3, 2))[q][k]
            row = rows_of[g % 4] + 24 * ((h + g // 4) % 2) + core * 3 + (ry // 3) * 6 + ry % 3
            mask = (lane8 < 64) if k == 0 else (lane8 >= 64)
            wide[pl.ds(base_s * STEP + row, 8, stride=STEP), :] = jnp.where(mask, second8, 0.0)
            wide[pl.ds(row, 8, stride=STEP), :] = jnp.where(mask, first8, 0.0)

    def exchange_copy(g):
        rows = pl.ds(g * 2 * NCH, 2 * NCH)
        return remote(ex_out.at[rows], ex_in.at[rows], ex_sem.at[g], ex_sem.at[8 + g], sibling)

    copies = {}

    def finish(g):
        @pl.when(t > 0)
        def _():
            halo_copy(g).wait_recv()
            half_f32[g * HR:(g + 1) * HR, :] = halo_in[g].astype(jnp.float32)

        @pl.when(t == 0)
        def _():
            half_f32[g * HR:(g + 1) * HR, :] = jnp.zeros((HR, 128), jnp.float32)

        for j in range(NCH):
            packed = half_f32[g * HR + j * S2:g * HR + (j + 1) * S2, :]
            by32, by64 = pltpu.roll(packed, 32, 1), pltpu.roll(packed, 64, 1)
            for q in range(2):
                index = 2 * (g * NCH + j) + q
                part = jnp.where(lane < 64, by64, by32) if q == 0 else jnp.where(lane < 64, by32, by64)
                v = main[index] + jnp.where(lane % 64 < 32, part, 0.0)
                v = v.astype(jnp.bfloat16).astype(jnp.float32)
                ex_out[index] = v[8:24].astype(jnp.bfloat16)
                widen(g, j, q, v[0:8], v[16:24], 8, c)
        copies[g] = start(exchange_copy(g))

    def accept(g):
        copies[g].wait_recv()
        for j in range(NCH):
            for q in range(2):
                v = ex_in[2 * (g * NCH + j) + q].astype(jnp.float32)
                widen(g, j, q, v[0:8], v[8:16], 4, 1 - c)

    def unit(g):
        compute(g)
        send_halo(g)

    round2(0)
    own_copy.wait()
    unit(0)
    round3(0)
    for n in (0, 1):
        for i in range(RC):
            z_second[2 * i + n].wait_recv()
        base(1, n)
    round4(0)
    unit(1)
    unit(2)
    round1(1)
    unit(3)
    finish(0)
    finish(1)
    round2(1)
    unit(4)
    finish(2)
    round3(1)
    finish(3)
    for g in range(4):
        accept(g)
    last(1, 1, 1)
    unit(5)
    last(1, 1, -1)
    unit(6)
    finish(4)
    last(1, 1, 2)
    for oa in (-1, 1, 2):
        last(1, 0, oa)
    unit(7)
    for g in (5, 6):
        finish(g)
    accept(4)
    finish(7)
    for g in (5, 6, 7):
        accept(g)

    both = lax.broadcasted_iota(jnp.int32, (TS, 128), 1) % TS == lax.broadcasted_iota(jnp.int32, (TS, 128), 0)
    both = jnp.where(both, 1.0, 0.0).astype(jnp.bfloat16)

    def turn(s, carry):
        block = wide[pl.ds(pl.multiple_of(s * STEP, 8), R), :].astype(jnp.bfloat16)
        out_ref[s] = lax.dot_general(both, block, (((1,), (1,)), ((), ())),
                                     preferred_element_type=jnp.float32).astype(jnp.bfloat16)
        return carry

    lax.fori_loop(0, SH, turn, 0)

    for copy in sends:
        copy.wait_send()

    @pl.when(t < NTM - 1)
    def _():
        for g in range(8):
            halo_copy(g).wait_send()


def body(shot_window, receiver_data, apertures, taper_index, taper_table):
    gathered = jnp.transpose(receiver_data, (1, 0, 2))
    vmem = pl.BlockSpec(memory_space=pltpu.VMEM)
    bf, f4 = jnp.bfloat16, jnp.float32
    dma = pltpu.SemaphoreType.DMA
    out = pl.pallas_call(
        kernel,
        out_shape=jax.ShapeDtypeStruct((SH, TS, R), bf),
        in_specs=[pl.BlockSpec(memory_space=pltpu.HBM)] * 5,
        out_specs=vmem,
        scratch_shapes=[
            pltpu.VMEM((2, NX, UR, ROWS, K), bf),
            pltpu.VMEM((2, RC, 32, K), bf),
            pltpu.VMEM((4, SH), jnp.int32),
            pltpu.VMEM((4, SH), jnp.int32),
            pltpu.SMEM((16,), f4),
            pltpu.VMEM((SH, LAG, K), bf),
            pltpu.VMEM((SH, LAG, K), bf),
            pltpu.VMEM((SH, LAG, K), bf),
            pltpu.VMEM((2, LAG * S2, 128), f4),
            pltpu.VMEM((LAG * SH, 2 * K), bf),
            pltpu.VMEM((NKB, 128), f4),
            pltpu.VMEM((LAG * SH, UR * WIN), f4),
            pltpu.VMEM((48, S2, 128), f4),
            pltpu.VMEM((8 * HR, 128), f4),
            pltpu.VMEM((8, HR, 128), bf),
            pltpu.VMEM((8, HR, 128), bf),
            pltpu.VMEM((48, 16, 128), bf),
            pltpu.VMEM((48, 16, 128), bf),
            pltpu.VMEM((16 * STEP, 128), f4),
            dma((NSEM,)), dma((NSEM,)), dma((4 * RC,)), dma((4 * RC,)), dma((2,)), dma((16,)), dma((16,)), dma((5,)),
        ],
        compiler_params=pltpu.CompilerParams(collective_id=0, has_side_effects=True,
                                             vmem_limit_bytes=60 * 1024 * 1024),
    )(gathered, shot_window, apertures.T, taper_index.T, taper_table)
    return jnp.transpose(out, (1, 0, 2))


def solution(mesh):
    in_specs = (P("shot", None, None), P("tm", "shot", None), P("shot", None), P("shot", None), P())
    out_specs = P("tm", "shot", None)
    return jax.shard_map(body, mesh=mesh, in_specs=in_specs, out_specs=out_specs, check_vma=False)
```

```python
import jax
import jax.numpy as jnp
from jax import lax
from jax.experimental import pallas as pl
from jax.experimental.pallas import tpu as pltpu
from jax.sharding import PartitionSpec as P

MESH = pl.DeviceIdType.MESH
NX, NY, NH, NC, NTM = 4, 4, 2, 2, 8
NZ = NH * NTM
NKB, LAG, K = 8, 32, 256
SH, RC, TS = 12, 3, 64
S2 = 2 * SH
UR = NY * RC
NCH = 3
R = 192
STEP = 200
HEAD, ROWS, WIN = 16, 112, 96
ORDER = (0, 1, 3, 2)
HR = 80
NSEM = 80

HALF = ((0, 32), (32, 32))
PLUS = ((16, 16), (32, 16))
MINUS = ((0, 16), (48, 16))


def device(x, y, h, c, t):
    return (((x * NH + h) * NY + y) * NC + c, t)


def kernel(x_ref, shot_hbm, aper_hbm, tidx_hbm, table_hbm, out_ref,
           xg, rz, aper_ref, tidx_ref, table_ref, shot_ref, op_own, op_sib, op_f32, op_all, wt, prod, main, half_f32, halo_out, halo_in,
           ex_out, ex_in, wide, result, send_sem, recv_sem, z_send, z_recv, op_sem, halo_sem, ex_sem, out_sem, local_sem):
    shot_i = lax.axis_index("shot")
    t = lax.axis_index("tm")
    c = shot_i % 2
    y = (shot_i // 2) % 4
    h = (shot_i // 8) % 2
    x = shot_i // 16
    z = h * NTM + t
    xs = [(x + d) % NX for d in range(NX)]
    ys = [RC * ((y + d) % NY) for d in range(NY)]
    zp = (z + 4) % NZ
    zm = (z + NZ - 4) % NZ
    up = device(x, y, zp // NTM, c, zp % NTM)
    down = device(x, y, zm // NTM, c, zm % NTM)
    sibling = device(x, y, h, 1 - c, t)
    after = device(x, y, h, c, (t + 1) % NTM)
    before = device(x, y, h, c, (t + NTM - 1) % NTM)
    near = {
        ("x", 1): device((x + 1) % NX, y, h, c, t),
        ("x", -1): device((x + NX - 1) % NX, y, h, c, t),
        ("y", 1): device(x, (y + 1) % NY, h, c, t),
        ("y", -1): device(x, (y + NY - 1) % NY, h, c, t),
    }
    partners = list(near.values()) + [up, down, sibling, after, before]

    barrier = pltpu.get_barrier_semaphore()
    for who in partners:
        pl.semaphore_signal(barrier, inc=1, device_id=who, device_id_type=MESH)
    own_copy = pltpu.make_async_copy(x_ref, xg.at[0, x, pl.ds(ys[0], RC), pl.ds(HEAD, TS)], local_sem.at[0])
    own_copy.start()
    shot_copy = pltpu.make_async_copy(shot_hbm, shot_ref, local_sem.at[1])
    shot_copy.start()
    small = [pltpu.make_async_copy(a, b, local_sem.at[2 + i])
             for i, (a, b) in enumerate(((aper_hbm, aper_ref), (tidx_hbm, tidx_ref), (table_hbm, table_ref)))]
    for copy in small:
        copy.start()

    pl.semaphore_wait(barrier, len(partners))

    sends = []
    kinds = {}

    def slot(l, dx, dy, rows):
        return xg.at[l, xs[dx % NX], pl.ds(ys[dy % NY], RC), pl.ds(HEAD + rows[0], rows[1])]

    def remote(src, dst, ssem, rsem, who):
        return pltpu.make_async_remote_copy(src_ref=src, dst_ref=dst, send_sem=ssem, recv_sem=rsem,
                                            device_id=who, device_id_type=MESH)

    def start(copy):
        copy.start()
        sends.append(copy)
        return copy

    def flush(keep):
        while len(sends) > keep:
            sends.pop(0).wait_send()

    z_first = [[start(remote(x_ref.at[pl.ds(i, 1), pl.ds(32 * d, 32)], rz.at[d, pl.ds(i, 1)],
                             z_send.at[2 * i + d], z_recv.at[2 * i + d], who))
                for d, who in ((0, up), (1, down))] for i in range(RC)]

    def send(l, n, oa, ob, rows, axis, way):
        first = "y" if n == 0 else "x"
        dx, dy = (ob, oa) if first == "y" else (oa, ob)
        step = way if axis == first else 0
        other = way if axis != first else 0
        key = (l, n, oa - step, ob - other, rows)
        k = kinds.setdefault(("sem",) + key + (axis, way), len([q for q in kinds if q[0] == "sem"]))
        ref = slot(l, dx, dy, rows)
        src = ref
        if l == 0 and oa == 0 and ob == 0:
            src = x_ref.at[:, pl.ds(rows[0], rows[1])]
        kinds[key] = start(remote(src, ref, send_sem.at[k], recv_sem.at[k], near[(axis, way)]))

    def recv(l, n, oa, ob, rows):
        kinds[(l, n, oa, ob, rows)].wait_recv()

    def axes(n):
        return ("y", "x") if n == 0 else ("x", "y")

    def base(l, n):
        a, b = axes(n)
        for axis in (a, b):
            for way in (1, -1):
                send(l, n, 0, 0, HALF[n], axis, way)

    def round1(l):
        for n in (0, 1):
            a, b = axes(n)
            for off, way, piece in ((-1, 1, PLUS), (1, -1, MINUS)):
                recv(l, n, off, 0, HALF[n])
                send(l, n, off, 0, piece[n], a, way)
                for w in (1, -1):
                    send(l, n, off, 0, HALF[n], b, w)
        for n in (0, 1):
            a, b = axes(n)
            for off, way, piece in ((-1, 1, PLUS), (1, -1, MINUS)):
                recv(l, n, 0, off, HALF[n])
                send(l, n, 0, off, piece[n], b, way)

    def round2(l):
        for n in (0, 1):
            a, b = axes(n)
            recv(l, n, -2, 0, PLUS[n])
            recv(l, n, 2, 0, MINUS[n])
            for w in (1, -1):
                send(l, n, 2, 0, HALF[n], b, w)
        for oa in (-1, 1):
            for n in (0, 1):
                a, b = axes(n)
                for off, way, piece in ((-1, 1, PLUS), (1, -1, MINUS)):
                    recv(l, n, oa, off, HALF[n])
                    send(l, n, oa, off, piece[n], b, way)
        for n in (0, 1):
            recv(l, n, 0, -2, PLUS[n])
            recv(l, n, 0, 2, MINUS[n])

    def round3(l):
        for n in (0, 1):
            a, b = axes(n)
            for off, way, piece in ((-1, 1, PLUS), (1, -1, MINUS)):
                recv(l, n, 2, off, HALF[n])
                send(l, n, 2, off, piece[n], b, way)

    def last(l, n, oa):
        recv(l, n, oa, -2, PLUS[n])
        recv(l, n, oa, 2, MINUS[n])

    def round4(l):
        for oa in (-1, 1, 2):
            for n in (0, 1):
                last(l, n, oa)

    base(0, 0)
    base(0, 1)

    for l in range(2):
        xg[l, :, :, 0:HEAD, :] = jnp.zeros((NX, UR, HEAD, K), jnp.bfloat16)
        xg[l, :, :, HEAD + TS:ROWS, :] = jnp.zeros((NX, UR, ROWS - HEAD - TS, K), jnp.bfloat16)
    half_f32[...] = jnp.zeros_like(half_f32)

    for copy in small:
        copy.wait()
    wt[...] = jnp.zeros_like(wt)
    tidx = tidx_ref[...]
    aper = aper_ref[...]
    picked = jnp.zeros(tidx.shape, jnp.float32)
    for j in range(16):
        picked = picked + jnp.where(tidx == j, table_ref[j], jnp.float32(0.0))
    for b in range(NKB):
        wt[b:b + 1, 0:SH] = jnp.sum(jnp.where(aper == b, picked, jnp.float32(0.0)), axis=0, keepdims=True)
    weight = wt[...].T
    block = lax.broadcasted_iota(jnp.int32, (16, K), 1) // (K // NKB)
    spread = jnp.zeros((16, K), jnp.float32)
    for b in range(NKB):
        spread = jnp.where(block == b, weight[0:16, b:b + 1], spread)
    shot_copy.wait()
    for s in range(SH):
        op_own[s] = (shot_ref[s].astype(jnp.float32) * spread[s:s + 1, :]).astype(jnp.bfloat16)
    op_copy = start(remote(op_own, op_sib, op_sem.at[0], op_sem.at[1], sibling))

    round1(0)
    z_second = []
    for i in range(RC):
        for d, who in ((0, up), (1, down)):
            z_first[i][d].wait_recv()
            dst = xg.at[1, x, pl.ds(ys[0] + i, 1), pl.ds(HEAD + HALF[d][0], 32)]
            k = 2 * (RC + i) + d
            z_second.append(start(remote(rz.at[d, pl.ds(i, 1)], dst, z_send.at[k], z_recv.at[k], who)))

    def place(ref, s, row):
        v = ref[s].astype(jnp.float32)
        for q in range(2):
            op_f32[q, pl.ds(row, LAG, stride=S2), :] = v[:, q * 128:(q + 1) * 128]

    for s in range(SH):
        place(op_own, s, s if s < 8 else 8 + s)
    op_copy.wait_recv()
    for s in range(SH):
        place(op_sib, s, 8 + s if s < 8 else 12 + s)
    for q in range(2):
        for a in range(2):
            cols = a * K + q * 128
            op_all[:, cols:cols + 128] = op_f32[q, a * LAG * SH:(a + 1) * LAG * SH, :].astype(jnp.bfloat16)

    lane = lax.broadcasted_iota(jnp.int32, (S2, 128), 1)

    def compute(g):
        l, ux = g // 4, xs[ORDER[g % 4]]
        for r0, nr in ((0, 8), (8, 4)):
            late = xg[l, ux, r0:r0 + nr, HEAD:HEAD + WIN, :].reshape(nr * WIN, K)
            early = xg[l, ux, r0:r0 + nr, 0:WIN, :].reshape(nr * WIN, K)
            prod[:, r0 * WIN:(r0 + nr) * WIN] = lax.dot_general(
                op_all[...], jnp.concatenate([late, early], axis=1), (((1,), (1,)), ((), ())),
                preferred_element_type=jnp.float32)
        for j in range(NCH):
            acc = prod[0:S2, j * 4 * WIN:(j + 1) * 4 * WIN]
            for b in range(1, LAG // 2):
                acc = acc + pltpu.roll(prod[b * S2:(b + 1) * S2, j * 4 * WIN:(j + 1) * 4 * WIN], b, 1)
            v0, v1, v2 = acc[:, 0:128], acc[:, 128:256], acc[:, 256:384]
            index = g * NCH + j
            main[2 * index] = jnp.where(lane < 64, v0, pltpu.roll(jnp.where(lane >= 96, v0, v1), 96, 1))
            main[2 * index + 1] = jnp.where(lane < 64, pltpu.roll(v2, 96, 1), v1)
            halo = jnp.where(lane < 32, v2, jnp.where(lane < 64, v1, jnp.where(lane < 96, v0, v2)))
            half_f32[g * HR + j * S2:g * HR + (j + 1) * S2, :] = halo

    def halo_copy(g):
        return remote(halo_out.at[g], halo_in.at[g], halo_sem.at[g], halo_sem.at[8 + g], after)

    def send_halo(g):
        halo_out[g] = half_f32[g * HR:(g + 1) * HR, :].astype(jnp.bfloat16)

        @pl.when(t < NTM - 1)
        def _():
            halo_copy(g).start()

    lane8 = lax.broadcasted_iota(jnp.int32, (8, 128), 1)

    rows_of = [xs[d] * 48 for d in ORDER]

    def widen(g, j, q, first8, second8, base_s, core):
        for k in range(2):
            ry = 4 * j + ((0, 1), (3, 2))[q][k]
            row = rows_of[g % 4] + 24 * ((h + g // 4) % 2) + core * 3 + (ry // 3) * 6 + ry % 3
            mask = (lane8 < 64) if k == 0 else (lane8 >= 64)
            wide[pl.ds(base_s * STEP + row, 8, stride=STEP), :] = jnp.where(mask, second8, 0.0)
            wide[pl.ds(row, 8, stride=STEP), :] = jnp.where(mask, first8, 0.0)

    def exchange_copy(g):
        rows = pl.ds(g * 2 * NCH, 2 * NCH)
        return remote(ex_out.at[rows], ex_in.at[rows], ex_sem.at[g], ex_sem.at[8 + g], sibling)

    copies = {}

    def finish(g):
        @pl.when(t > 0)
        def _():
            halo_copy(g).wait_recv()
            half_f32[g * HR:(g + 1) * HR, :] = halo_in[g].astype(jnp.float32)

        @pl.when(t == 0)
        def _():
            half_f32[g * HR:(g + 1) * HR, :] = jnp.zeros((HR, 128), jnp.float32)

        for j in range(NCH):
            packed = half_f32[g * HR + j * S2:g * HR + (j + 1) * S2, :]
            by32, by64 = pltpu.roll(packed, 32, 1), pltpu.roll(packed, 64, 1)
            for q in range(2):
                index = 2 * (g * NCH + j) + q
                part = jnp.where(lane < 64, by64, by32) if q == 0 else jnp.where(lane < 64, by32, by64)
                v = main[index] + jnp.where(lane % 64 < 32, part, 0.0)
                v = v.astype(jnp.bfloat16).astype(jnp.float32)
                ex_out[index] = v[8:24].astype(jnp.bfloat16)
                widen(g, j, q, v[0:8], v[16:24], 8, c)
        copies[g] = start(exchange_copy(g))

    def accept(g):
        copies[g].wait_recv()
        for j in range(NCH):
            for q in range(2):
                v = ex_in[2 * (g * NCH + j) + q].astype(jnp.float32)
                widen(g, j, q, v[0:8], v[8:16], 4, 1 - c)

    def unit(g):
        compute(g)
        send_halo(g)

    round2(0)
    own_copy.wait()
    unit(0)
    round3(0)
    for n in (0, 1):
        for i in range(RC):
            z_second[2 * i + n].wait_recv()
        base(1, n)
    round4(0)
    unit(1)
    unit(2)
    round1(1)
    unit(3)
    finish(0)
    finish(1)
    round2(1)
    unit(4)
    finish(2)
    flush(20)
    round3(1)
    finish(3)
    for g in range(4):
        accept(g)
    flush(8)
    last(1, 1, 1)
    unit(5)
    last(1, 1, -1)
    unit(6)
    finish(4)
    last(1, 1, 2)
    for oa in (-1, 1, 2):
        last(1, 0, oa)
    unit(7)
    for g in (5, 6):
        finish(g)
    accept(4)
    finish(7)
    for g in (5, 6, 7):
        accept(g)

    both = lax.broadcasted_iota(jnp.int32, (TS, 128), 1) % TS == lax.broadcasted_iota(jnp.int32, (TS, 128), 0)
    both = jnp.where(both, 1.0, 0.0).astype(jnp.bfloat16)

    leaving = []
    for s in range(SH):
        block = wide[s * STEP:s * STEP + R, :].astype(jnp.bfloat16)
        result[s] = lax.dot_general(both, block, (((1,), (1,)), ((), ())),
                                    preferred_element_type=jnp.float32).astype(jnp.bfloat16)
        copy = pltpu.make_async_copy(result.at[s], out_ref.at[s], out_sem.at[s])
        copy.start()
        leaving.append(copy)

    flush(0)
    for copy in leaving:
        copy.wait()

    @pl.when(t < NTM - 1)
    def _():
        for g in range(8):
            halo_copy(g).wait_send()


def body(shot_window, receiver_data, apertures, taper_index, taper_table):
    gathered = jnp.transpose(receiver_data, (1, 0, 2))
    bf, f4 = jnp.bfloat16, jnp.float32
    dma = pltpu.SemaphoreType.DMA
    out = pl.pallas_call(
        kernel,
        out_shape=jax.ShapeDtypeStruct((SH, TS, R), bf),
        in_specs=[pl.BlockSpec(memory_space=pltpu.HBM)] * 5,
        out_specs=pl.BlockSpec(memory_space=pl.ANY),
        scratch_shapes=[
            pltpu.VMEM((2, NX, UR, ROWS, K), bf),
            pltpu.VMEM((2, RC, 32, K), bf),
            pltpu.VMEM((4, SH), jnp.int32),
            pltpu.VMEM((4, SH), jnp.int32),
            pltpu.SMEM((16,), f4),
            pltpu.VMEM((SH, LAG, K), bf),
            pltpu.VMEM((SH, LAG, K), bf),
            pltpu.VMEM((SH, LAG, K), bf),
            pltpu.VMEM((2, LAG * S2, 128), f4),
            pltpu.VMEM((LAG * SH, 2 * K), bf),
            pltpu.VMEM((NKB, 128), f4),
            pltpu.VMEM((LAG * SH, UR * WIN), f4),
            pltpu.VMEM((48, S2, 128), f4),
            pltpu.VMEM((8 * HR, 128), f4),
            pltpu.VMEM((8, HR, 128), bf),
            pltpu.VMEM((8, HR, 128), bf),
            pltpu.VMEM((48, 16, 128), bf),
            pltpu.VMEM((48, 16, 128), bf),
            pltpu.VMEM((16 * STEP, 128), f4),
            pltpu.VMEM((SH, TS, R), bf),
            dma((NSEM,)), dma((NSEM,)), dma((4 * RC,)), dma((4 * RC,)), dma((2,)), dma((16,)), dma((16,)), dma((SH,)), dma((5,)),
        ],
        compiler_params=pltpu.CompilerParams(collective_id=0, has_side_effects=True,
                                             vmem_limit_bytes=60 * 1024 * 1024),
    )(gathered, shot_window, apertures.T, taper_index.T, taper_table)
    return jnp.transpose(out, (1, 0, 2))


def solution(mesh):
    in_specs = (P("shot", None, None), P("tm", "shot", None), P("shot", None), P("shot", None), P())
    out_specs = P("tm", "shot", None)
    return jax.shard_map(body, mesh=mesh, in_specs=in_specs, out_specs=out_specs, check_vma=False)
```

```python
import jax
import jax.numpy as jnp
from jax import lax
from jax.experimental import pallas as pl
from jax.experimental.pallas import tpu as pltpu
from jax.sharding import PartitionSpec as P

MESH = pl.DeviceIdType.MESH
NX, NY, NH, NC, NTM = 4, 4, 2, 2, 8
NZ = NH * NTM
NKB, LAG, K = 8, 32, 256
SH, RC, TS = 12, 3, 64
S2 = 2 * SH
UR = NY * RC
NCH = 3
R = 192
STEP = 200
HEAD, ROWS, WIN = 16, 112, 96
ORDER = (0, 1, 3, 2)
HR = 80
NSEM = 80

HALF = ((0, 32), (32, 32))
PLUS = ((16, 16), (32, 16))
MINUS = ((0, 16), (48, 16))


def device(x, y, h, c, t):
    return (((x * NH + h) * NY + y) * NC + c, t)


def kernel(x_ref, shot_hbm, aper_hbm, tidx_hbm, table_hbm, out_ref,
           xg, rz, aper_ref, tidx_ref, table_ref, shot_ref, op_own, op_sib, op_f32, op_all, wt, prod, main, half_f32, halo_out, halo_in,
           ex_out, ex_in, wide, result, send_sem, recv_sem, z_send, z_recv, op_sem, halo_sem, ex_sem, out_sem, local_sem):
    shot_i = lax.axis_index("shot")
    t = lax.axis_index("tm")
    c = shot_i % 2
    y = (shot_i // 2) % 4
    h = (shot_i // 8) % 2
    x = shot_i // 16
    z = h * NTM + t
    xs = [(x + d) % NX for d in range(NX)]
    ys = [(y + d) % NY for d in range(NY)]
    zp = (z + 4) % NZ
    zm = (z + NZ - 4) % NZ
    up = device(x, y, zp // NTM, c, zp % NTM)
    down = device(x, y, zm // NTM, c, zm % NTM)
    sibling = device(x, y, h, 1 - c, t)
    after = device(x, y, h, c, (t + 1) % NTM)
    before = device(x, y, h, c, (t + NTM - 1) % NTM)
    near = {
        ("x", 1): device((x + 1) % NX, y, h, c, t),
        ("x", -1): device((x + NX - 1) % NX, y, h, c, t),
        ("y", 1): device(x, (y + 1) % NY, h, c, t),
        ("y", -1): device(x, (y + NY - 1) % NY, h, c, t),
    }
    cross_after = device(x, y, h, 1 - c, (t + 1) % NTM)
    cross_before = device(x, y, h, 1 - c, (t + NTM - 1) % NTM)
    partners = list(near.values()) + [up, down, sibling, after, before, cross_after, cross_before]

    barrier = pltpu.get_barrier_semaphore()
    for who in partners:
        pl.semaphore_signal(barrier, inc=1, device_id=who, device_id_type=MESH)
    own_copy = pltpu.make_async_copy(x_ref, xg.at[0, 0, pl.ds(0, RC), pl.ds(HEAD, TS)], local_sem.at[0])
    own_copy.start()
    shot_copy = pltpu.make_async_copy(shot_hbm, shot_ref, local_sem.at[1])
    shot_copy.start()
    small = [pltpu.make_async_copy(a, b, local_sem.at[2 + i])
             for i, (a, b) in enumerate(((aper_hbm, aper_ref), (tidx_hbm, tidx_ref), (table_hbm, table_ref)))]
    for copy in small:
        copy.start()

    pl.semaphore_wait(barrier, len(partners))

    sends = []
    kinds = {}

    def slot(l, dx, dy, rows):
        return xg.at[l, dx % NX, pl.ds(RC * (dy % NY), RC), pl.ds(HEAD + rows[0], rows[1])]

    def remote(src, dst, ssem, rsem, who):
        return pltpu.make_async_remote_copy(src_ref=src, dst_ref=dst, send_sem=ssem, recv_sem=rsem,
                                            device_id=who, device_id_type=MESH)

    def start(copy):
        copy.start()
        sends.append(copy)
        return copy

    def flush(keep):
        while len(sends) > keep:
            sends.pop(0).wait_send()

    z_first = [[start(remote(x_ref.at[pl.ds(i, 1), pl.ds(32 * d, 32)], rz.at[d, pl.ds(i, 1)],
                             z_send.at[2 * i + d], z_recv.at[2 * i + d], who))
                for d, who in ((0, up), (1, down))] for i in range(RC)]

    def send(l, n, oa, ob, rows, axis, way):
        first = "y" if n == 0 else "x"
        dx, dy = (ob, oa) if first == "y" else (oa, ob)
        step = way if axis == first else 0
        other = way if axis != first else 0
        key = (l, n, oa - step, ob - other, rows)
        k = kinds.setdefault(("sem",) + key + (axis, way), len([q for q in kinds if q[0] == "sem"]))
        src = slot(l, dx, dy, rows)
        if l == 0 and oa == 0 and ob == 0:
            src = x_ref.at[:, pl.ds(rows[0], rows[1])]
        back = (-way, 0) if axis == "x" else (0, -way)
        dst = slot(l, dx + back[0], dy + back[1], rows)
        kinds[key] = start(remote(src, dst, send_sem.at[k], recv_sem.at[k], near[(axis, way)]))

    def recv(l, n, oa, ob, rows):
        kinds[(l, n, oa, ob, rows)].wait_recv()

    def axes(n):
        return ("y", "x") if n == 0 else ("x", "y")

    def base(l, n):
        a, b = axes(n)
        for axis in (a, b):
            for way in (1, -1):
                send(l, n, 0, 0, HALF[n], axis, way)

    def round1(l):
        for n in (0, 1):
            a, b = axes(n)
            for off, way, piece in ((-1, 1, PLUS), (1, -1, MINUS)):
                recv(l, n, off, 0, HALF[n])
                send(l, n, off, 0, piece[n], a, way)
                for w in (1, -1):
                    send(l, n, off, 0, HALF[n], b, w)
        for n in (0, 1):
            a, b = axes(n)
            for off, way, piece in ((-1, 1, PLUS), (1, -1, MINUS)):
                recv(l, n, 0, off, HALF[n])
                send(l, n, 0, off, piece[n], b, way)

    def round2(l):
        for n in (0, 1):
            a, b = axes(n)
            recv(l, n, -2, 0, PLUS[n])
            recv(l, n, 2, 0, MINUS[n])
            for w in (1, -1):
                send(l, n, 2, 0, HALF[n], b, w)
        for oa in (-1, 1):
            for n in (0, 1):
                a, b = axes(n)
                for off, way, piece in ((-1, 1, PLUS), (1, -1, MINUS)):
                    recv(l, n, oa, off, HALF[n])
                    send(l, n, oa, off, piece[n], b, way)
        for n in (0, 1):
            recv(l, n, 0, -2, PLUS[n])
            recv(l, n, 0, 2, MINUS[n])

    def round3(l):
        for n in (0, 1):
            a, b = axes(n)
            for off, way, piece in ((-1, 1, PLUS), (1, -1, MINUS)):
                recv(l, n, 2, off, HALF[n])
                send(l, n, 2, off, piece[n], b, way)

    def last(l, n, oa):
        recv(l, n, oa, -2, PLUS[n])
        recv(l, n, oa, 2, MINUS[n])

    def round4(l):
        for oa in (-1, 1, 2):
            for n in (0, 1):
                last(l, n, oa)

    base(0, 0)
    base(0, 1)

    for l in range(2):
        xg[l, :, :, 0:HEAD, :] = jnp.zeros((NX, UR, HEAD, K), jnp.bfloat16)
        xg[l, :, :, HEAD + TS:ROWS, :] = jnp.zeros((NX, UR, ROWS - HEAD - TS, K), jnp.bfloat16)
    half_f32[...] = jnp.zeros_like(half_f32)

    @pl.when(t == 0)
    def _():
        halo_in[...] = jnp.zeros_like(halo_in)

    for copy in small:
        copy.wait()
    wt[...] = jnp.zeros_like(wt)
    tidx = tidx_ref[...]
    aper = aper_ref[...]
    picked = jnp.zeros(tidx.shape, jnp.float32)
    for j in range(16):
        picked = picked + jnp.where(tidx == j, table_ref[j], jnp.float32(0.0))
    for b in range(NKB):
        wt[b:b + 1, 0:SH] = jnp.sum(jnp.where(aper == b, picked, jnp.float32(0.0)), axis=0, keepdims=True)
    weight = wt[...].T
    block = lax.broadcasted_iota(jnp.int32, (16, K), 1) // (K // NKB)
    spread = jnp.zeros((16, K), jnp.float32)
    for b in range(NKB):
        spread = jnp.where(block == b, weight[0:16, b:b + 1], spread)
    shot_copy.wait()
    for s in range(SH):
        op_own[s] = (shot_ref[s].astype(jnp.float32) * spread[s:s + 1, :]).astype(jnp.bfloat16)
    op_copy = start(remote(op_own, op_sib, op_sem.at[0], op_sem.at[1], sibling))

    round1(0)
    z_second = []
    for i in range(RC):
        for d, who in ((0, up), (1, down)):
            z_first[i][d].wait_recv()
            dst = xg.at[1, 0, pl.ds(i, 1), pl.ds(HEAD + HALF[d][0], 32)]
            k = 2 * (RC + i) + d
            z_second.append(start(remote(rz.at[d, pl.ds(i, 1)], dst, z_send.at[k], z_recv.at[k], who)))

    def place(ref, s, row):
        v = ref[s].astype(jnp.float32)
        for q in range(2):
            op_f32[q, pl.ds(row, LAG, stride=S2), :] = v[:, q * 128:(q + 1) * 128]

    for s in range(SH):
        place(op_own, s, s if s < 8 else 8 + s)
    op_copy.wait_recv()
    for s in range(SH):
        place(op_sib, s, 8 + s if s < 8 else 12 + s)
    for q in range(2):
        for a in range(2):
            cols = a * K + q * 128
            op_all[:, cols:cols + 128] = op_f32[q, a * LAG * SH:(a + 1) * LAG * SH, :].astype(jnp.bfloat16)

    lane = lax.broadcasted_iota(jnp.int32, (S2, 128), 1)

    def compute(g):
        l, ux = g // 4, ORDER[g % 4]
        for r0, nr in ((0, 8), (8, 4)):
            late = xg[l, ux, r0:r0 + nr, HEAD:HEAD + WIN, :].reshape(nr * WIN, K)
            early = xg[l, ux, r0:r0 + nr, 0:WIN, :].reshape(nr * WIN, K)
            prod[:, r0 * WIN:(r0 + nr) * WIN] = lax.dot_general(
                op_all[...], jnp.concatenate([late, early], axis=1), (((1,), (1,)), ((), ())),
                preferred_element_type=jnp.float32)
        for j in range(NCH):
            acc = prod[0:S2, j * 4 * WIN:(j + 1) * 4 * WIN]
            for b in range(1, LAG // 2):
                acc = acc + pltpu.roll(prod[b * S2:(b + 1) * S2, j * 4 * WIN:(j + 1) * 4 * WIN], b, 1)
            v0, v1, v2 = acc[:, 0:128], acc[:, 128:256], acc[:, 256:384]
            index = g * NCH + j
            pairs = (jnp.where(lane < 64, v0, pltpu.roll(jnp.where(lane >= 96, v0, v1), 96, 1)),
                     jnp.where(lane < 64, pltpu.roll(v2, 96, 1), v1))
            for q in range(2):
                main[2 * index + q] = pairs[q]
                ex_out[2 * index + q] = pairs[q][8:24]
            halo = jnp.where(lane < 32, v2, jnp.where(lane < 64, v1, jnp.where(lane < 96, v0, v2)))
            half_f32[g * HR + j * S2:g * HR + (j + 1) * S2, :] = halo

    def halo_copy(g, k):
        return remote(halo_out.at[g], halo_in.at[k, g], halo_sem.at[16 * k + g], halo_sem.at[16 * k + 8 + g],
                      (after, cross_after)[k])

    def send_halo(g):
        halo_out[g] = half_f32[g * HR:(g + 1) * HR, :].astype(jnp.bfloat16)

        @pl.when(t < NTM - 1)
        def _():
            for k in range(2):
                halo_copy(g, k).start()

    lane8 = lax.broadcasted_iota(jnp.int32, (8, 128), 1)

    rows_of = [xs[d] * 48 for d in ORDER]

    def widen(g, j, q, first8, second8, base_s, core):
        for k in range(2):
            ry = 4 * j + ((0, 1), (3, 2))[q][k]
            row = rows_of[g % 4] + 24 * ((h + g // 4) % 2) + core * 3 + 6 * ys[ry // 3] + ry % 3
            mask = (lane8 < 64) if k == 0 else (lane8 >= 64)
            wide[pl.ds(base_s * STEP + row, 8, stride=STEP), :] = jnp.where(mask, second8, 0.0)
            wide[pl.ds(row, 8, stride=STEP), :] = jnp.where(mask, first8, 0.0)

    def exchange_copy(g):
        rows = pl.ds(g * 2 * NCH, 2 * NCH)
        return remote(ex_out.at[rows], ex_in.at[rows], ex_sem.at[g], ex_sem.at[8 + g], sibling)

    copies = {}

    def close(g):
        @pl.when(t > 0)
        def _():
            for k in range(2):
                halo_copy(g, k).wait_recv()

        copies[g].wait_recv()
        for k in range(2):
            halo = halo_in[k, g].astype(jnp.float32)
            for j in range(NCH):
                packed = halo[j * S2 + 8 * k:(j + 1) * S2]
                place = lane[8 * k:]
                by32, by64 = pltpu.roll(packed, 32, 1), pltpu.roll(packed, 64, 1)
                for q in range(2):
                    index = 2 * (g * NCH + j) + q
                    part = jnp.where(place < 64, by64, by32) if q == 0 else jnp.where(place < 64, by32, by64)
                    v = (main, ex_in)[k][index] + jnp.where(place % 64 < 32, part, 0.0)
                    if k == 0:
                        widen(g, j, q, v[0:8], v[16:24], 8, c)
                    else:
                        widen(g, j, q, v[0:8], v[8:16], 4, 1 - c)

    def unit(g):
        compute(g)
        send_halo(g)
        copies[g] = start(exchange_copy(g))

    round2(0)
    own_copy.wait()
    unit(0)
    round3(0)
    for n in (0, 1):
        for i in range(RC):
            z_second[2 * i + n].wait_recv()
        base(1, n)
    round4(0)
    unit(1)
    unit(2)
    round1(1)
    unit(3)
    close(0)
    close(1)
    round2(1)
    unit(4)
    close(2)
    flush(20)
    round3(1)
    close(3)
    flush(8)
    last(1, 1, 1)
    unit(5)
    last(1, 1, -1)
    unit(6)
    close(4)
    last(1, 1, 2)
    for oa in (-1, 1, 2):
        last(1, 0, oa)
    unit(7)
    for g in (5, 6, 7):
        close(g)

    both = lax.broadcasted_iota(jnp.int32, (TS, 128), 1) % TS == lax.broadcasted_iota(jnp.int32, (TS, 128), 0)
    both = jnp.where(both, 1.0, 0.0).astype(jnp.bfloat16)

    leaving = []
    for s in range(SH):
        block = wide[s * STEP:s * STEP + R, :].astype(jnp.bfloat16)
        result[s] = lax.dot_general(both, block, (((1,), (1,)), ((), ())),
                                    preferred_element_type=jnp.float32).astype(jnp.bfloat16)
        copy = pltpu.make_async_copy(result.at[s], out_ref.at[s], out_sem.at[s])
        copy.start()
        leaving.append(copy)

    flush(0)
    for copy in leaving:
        copy.wait()

    @pl.when(t < NTM - 1)
    def _():
        for g in range(8):
            for k in range(2):
                halo_copy(g, k).wait_send()


def body(shot_window, receiver_data, apertures, taper_index, taper_table):
    gathered = jnp.transpose(receiver_data, (1, 0, 2))
    bf, f4 = jnp.bfloat16, jnp.float32
    dma = pltpu.SemaphoreType.DMA
    out = pl.pallas_call(
        kernel,
        out_shape=jax.ShapeDtypeStruct((SH, TS, R), bf),
        in_specs=[pl.BlockSpec(memory_space=pltpu.HBM)] * 5,
        out_specs=pl.BlockSpec(memory_space=pl.ANY),
        scratch_shapes=[
            pltpu.VMEM((2, NX, UR, ROWS, K), bf),
            pltpu.VMEM((2, RC, 32, K), bf),
            pltpu.VMEM((4, SH), jnp.int32),
            pltpu.VMEM((4, SH), jnp.int32),
            pltpu.SMEM((16,), f4),
            pltpu.VMEM((SH, LAG, K), bf),
            pltpu.VMEM((SH, LAG, K), bf),
            pltpu.VMEM((SH, LAG, K), bf),
            pltpu.VMEM((2, LAG * S2, 128), f4),
            pltpu.VMEM((LAG * SH, 2 * K), bf),
            pltpu.VMEM((NKB, 128), f4),
            pltpu.VMEM((LAG * SH, UR * WIN), f4),
            pltpu.VMEM((48, S2, 128), f4),
            pltpu.VMEM((8 * HR, 128), f4),
            pltpu.VMEM((8, HR, 128), bf),
            pltpu.VMEM((2, 8, HR, 128), bf),
            pltpu.VMEM((48, 16, 128), f4),
            pltpu.VMEM((48, 16, 128), f4),
            pltpu.VMEM((16 * STEP, 128), f4),
            pltpu.VMEM((SH, TS, R), bf),
            dma((NSEM,)), dma((NSEM,)), dma((4 * RC,)), dma((4 * RC,)), dma((2,)), dma((32,)), dma((16,)), dma((SH,)), dma((5,)),
        ],
        compiler_params=pltpu.CompilerParams(collective_id=0, has_side_effects=True,
                                             vmem_limit_bytes=60 * 1024 * 1024),
    )(gathered, shot_window, apertures.T, taper_index.T, taper_table)
    return jnp.transpose(out, (1, 0, 2))


def solution(mesh):
    in_specs = (P("shot", None, None), P("tm", "shot", None), P("shot", None), P("shot", None), P())
    out_specs = P("tm", "shot", None)
    return jax.shard_map(body, mesh=mesh, in_specs=in_specs, out_specs=out_specs, check_vma=False)
```

```python
import jax
import jax.numpy as jnp
from jax import lax
from jax.experimental import pallas as pl
from jax.experimental.pallas import tpu as pltpu
from jax.sharding import PartitionSpec as P

MESH = pl.DeviceIdType.MESH
NX, NY, NH, NC, NTM = 4, 4, 2, 2, 8
NZ = NH * NTM
NKB, LAG, K = 8, 32, 256
SH, RC, TS = 12, 3, 64
S2 = 2 * SH
UR = NY * RC
NCH = 3
R = 192
STEP = 200
HEAD, ROWS, WIN = 16, 112, 96
ORDER = (0, 1, 3, 2)
HR = 80
NSEM = 80

HALF = ((0, 32), (32, 32))
PLUS = ((16, 16), (32, 16))
MINUS = ((0, 16), (48, 16))


def device(x, y, h, c, t):
    return (((x * NH + h) * NY + y) * NC + c, t)


def kernel(x_ref, shot_hbm, aper_hbm, tidx_hbm, table_hbm, out_ref,
           xg, rz, aper_ref, tidx_ref, table_ref, shot_ref, op_own, op_sib, op_f32, op_all, wt, prod, main, half_f32, halo_out, halo_in,
           ex_out, ex_in, wide, result, send_sem, recv_sem, z_send, z_recv, op_sem, halo_sem, ex_sem, out_sem, local_sem):
    shot_i = lax.axis_index("shot")
    t = lax.axis_index("tm")
    c = shot_i % 2
    y = (shot_i // 2) % 4
    h = (shot_i // 8) % 2
    x = shot_i // 16
    z = h * NTM + t
    xs = [(x + d) % NX for d in range(NX)]
    ys = [(y + d) % NY for d in range(NY)]
    zp = (z + 4) % NZ
    zm = (z + NZ - 4) % NZ
    up = device(x, y, zp // NTM, c, zp % NTM)
    down = device(x, y, zm // NTM, c, zm % NTM)
    sibling = device(x, y, h, 1 - c, t)
    after = device(x, y, h, c, (t + 1) % NTM)
    before = device(x, y, h, c, (t + NTM - 1) % NTM)
    near = {
        ("x", 1): device((x + 1) % NX, y, h, c, t),
        ("x", -1): device((x + NX - 1) % NX, y, h, c, t),
        ("y", 1): device(x, (y + 1) % NY, h, c, t),
        ("y", -1): device(x, (y + NY - 1) % NY, h, c, t),
    }
    cross_after = device(x, y, h, 1 - c, (t + 1) % NTM)
    cross_before = device(x, y, h, 1 - c, (t + NTM - 1) % NTM)
    partners = list(near.values()) + [up, down, sibling, after, before, cross_after, cross_before]

    barrier = pltpu.get_barrier_semaphore()
    for who in partners:
        pl.semaphore_signal(barrier, inc=1, device_id=who, device_id_type=MESH)
    own_copy = pltpu.make_async_copy(x_ref, xg.at[0, 0, pl.ds(0, RC), pl.ds(HEAD, TS)], local_sem.at[0])
    own_copy.start()
    shot_copy = pltpu.make_async_copy(shot_hbm, shot_ref, local_sem.at[1])
    shot_copy.start()
    small = [pltpu.make_async_copy(a, b, local_sem.at[2 + i])
             for i, (a, b) in enumerate(((aper_hbm, aper_ref), (tidx_hbm, tidx_ref), (table_hbm, table_ref)))]
    for copy in small:
        copy.start()

    pl.semaphore_wait(barrier, len(partners))

    sends = []
    kinds = {}

    def slot(l, dx, dy, rows):
        return xg.at[l, dx % NX, pl.ds(RC * (dy % NY), RC), pl.ds(HEAD + rows[0], rows[1])]

    def remote(src, dst, ssem, rsem, who):
        return pltpu.make_async_remote_copy(src_ref=src, dst_ref=dst, send_sem=ssem, recv_sem=rsem,
                                            device_id=who, device_id_type=MESH)

    def start(copy):
        copy.start()
        sends.append(copy)
        return copy

    def flush(keep):
        while len(sends) > keep:
            sends.pop(0).wait_send()

    z_first = [[start(remote(x_ref.at[pl.ds(i, 1), pl.ds(32 * d, 32)], rz.at[d, pl.ds(i, 1)],
                             z_send.at[2 * i + d], z_recv.at[2 * i + d], who))
                for d, who in ((0, up), (1, down))] for i in range(RC)]

    def send(l, n, oa, ob, rows, axis, way):
        first = "y" if n == 0 else "x"
        dx, dy = (ob, oa) if first == "y" else (oa, ob)
        step = way if axis == first else 0
        other = way if axis != first else 0
        key = (l, n, oa - step, ob - other, rows)
        k = kinds.setdefault(("sem",) + key + (axis, way), len([q for q in kinds if q[0] == "sem"]))
        src = slot(l, dx, dy, rows)
        if l == 0 and oa == 0 and ob == 0:
            src = x_ref.at[:, pl.ds(rows[0], rows[1])]
        back = (-way, 0) if axis == "x" else (0, -way)
        dst = slot(l, dx + back[0], dy + back[1], rows)
        kinds[key] = start(remote(src, dst, send_sem.at[k], recv_sem.at[k], near[(axis, way)]))

    def recv(l, n, oa, ob, rows):
        kinds[(l, n, oa, ob, rows)].wait_recv()

    def axes(n):
        return ("y", "x") if n == 0 else ("x", "y")

    def base(l, n):
        a, b = axes(n)
        for axis in (a, b):
            for way in (1, -1):
                send(l, n, 0, 0, HALF[n], axis, way)

    def round1(l):
        for n in (0, 1):
            a, b = axes(n)
            for off, way, piece in ((-1, 1, PLUS), (1, -1, MINUS)):
                recv(l, n, off, 0, HALF[n])
                send(l, n, off, 0, piece[n], a, way)
                for w in (1, -1):
                    send(l, n, off, 0, HALF[n], b, w)
        for n in (0, 1):
            a, b = axes(n)
            for off, way, piece in ((-1, 1, PLUS), (1, -1, MINUS)):
                recv(l, n, 0, off, HALF[n])
                send(l, n, 0, off, piece[n], b, way)

    def round2(l):
        for n in (0, 1):
            a, b = axes(n)
            recv(l, n, -2, 0, PLUS[n])
            recv(l, n, 2, 0, MINUS[n])
            for w in (1, -1):
                send(l, n, 2, 0, HALF[n], b, w)
        for oa in (-1, 1):
            for n in (0, 1):
                a, b = axes(n)
                for off, way, piece in ((-1, 1, PLUS), (1, -1, MINUS)):
                    recv(l, n, oa, off, HALF[n])
                    send(l, n, oa, off, piece[n], b, way)
        for n in (0, 1):
            recv(l, n, 0, -2, PLUS[n])
            recv(l, n, 0, 2, MINUS[n])

    def round3(l):
        for n in (0, 1):
            a, b = axes(n)
            for off, way, piece in ((-1, 1, PLUS), (1, -1, MINUS)):
                recv(l, n, 2, off, HALF[n])
                send(l, n, 2, off, piece[n], b, way)

    def last(l, n, oa):
        recv(l, n, oa, -2, PLUS[n])
        recv(l, n, oa, 2, MINUS[n])

    def round4(l):
        for oa in (-1, 1, 2):
            for n in (0, 1):
                last(l, n, oa)

    base(0, 0)
    base(0, 1)

    for l in range(2):
        xg[l, :, :, 0:HEAD, :] = jnp.zeros((NX, UR, HEAD, K), jnp.bfloat16)
        xg[l, :, :, HEAD + TS:ROWS, :] = jnp.zeros((NX, UR, ROWS - HEAD - TS, K), jnp.bfloat16)
    half_f32[...] = jnp.zeros_like(half_f32)

    @pl.when(t == 0)
    def _():
        halo_in[...] = jnp.zeros_like(halo_in)

    for copy in small:
        copy.wait()
    wt[...] = jnp.zeros_like(wt)
    tidx = tidx_ref[...]
    aper = aper_ref[...]
    picked = jnp.zeros(tidx.shape, jnp.float32)
    for j in range(16):
        picked = picked + jnp.where(tidx == j, table_ref[j], jnp.float32(0.0))
    for b in range(NKB):
        wt[b:b + 1, 0:SH] = jnp.sum(jnp.where(aper == b, picked, jnp.float32(0.0)), axis=0, keepdims=True)
    weight = wt[...].T
    block = lax.broadcasted_iota(jnp.int32, (16, K), 1) // (K // NKB)
    spread = jnp.zeros((16, K), jnp.float32)
    for b in range(NKB):
        spread = jnp.where(block == b, weight[0:16, b:b + 1], spread)
    shot_copy.wait()
    for s in range(SH):
        op_own[s] = (shot_ref[s].astype(jnp.float32) * spread[s:s + 1, :]).astype(jnp.bfloat16)
    op_copy = start(remote(op_own, op_sib, op_sem.at[0], op_sem.at[1], sibling))

    z_second = []

    def relay(i):
        for d, who in ((0, up), (1, down)):
            z_first[i][d].wait_recv()
            dst = xg.at[1, 0, pl.ds(i, 1), pl.ds(HEAD + HALF[d][0], 32)]
            k = 2 * (RC + i) + d
            z_second.append(start(remote(rz.at[d, pl.ds(i, 1)], dst, z_send.at[k], z_recv.at[k], who)))

    relay(0)
    round1(0)
    relay(1)
    relay(2)

    def place(ref, s, row):
        v = ref[s].astype(jnp.float32)
        for q in range(2):
            op_f32[q, pl.ds(row, LAG, stride=S2), :] = v[:, q * 128:(q + 1) * 128]

    for s in range(SH):
        place(op_own, s, s if s < 8 else 8 + s)
    op_copy.wait_recv()
    for s in range(SH):
        place(op_sib, s, 8 + s if s < 8 else 12 + s)
    for q in range(2):
        for a in range(2):
            cols = a * K + q * 128
            op_all[:, cols:cols + 128] = op_f32[q, a * LAG * SH:(a + 1) * LAG * SH, :].astype(jnp.bfloat16)

    lane = lax.broadcasted_iota(jnp.int32, (S2, 128), 1)

    def compute(g):
        l, ux = g // 4, ORDER[g % 4]
        for r0, nr in ((0, 8), (8, 4)):
            late = xg[l, ux, r0:r0 + nr, HEAD:HEAD + WIN, :].reshape(nr * WIN, K)
            early = xg[l, ux, r0:r0 + nr, 0:WIN, :].reshape(nr * WIN, K)
            prod[:, r0 * WIN:(r0 + nr) * WIN] = lax.dot_general(
                op_all[...], jnp.concatenate([late, early], axis=1), (((1,), (1,)), ((), ())),
                preferred_element_type=jnp.float32)
        for j in range(NCH):
            acc = prod[0:S2, j * 4 * WIN:(j + 1) * 4 * WIN]
            for b in range(1, LAG // 2):
                acc = acc + pltpu.roll(prod[b * S2:(b + 1) * S2, j * 4 * WIN:(j + 1) * 4 * WIN], b, 1)
            v0, v1, v2 = acc[:, 0:128], acc[:, 128:256], acc[:, 256:384]
            index = g * NCH + j
            pairs = (jnp.where(lane < 64, v0, pltpu.roll(jnp.where(lane >= 96, v0, v1), 96, 1)),
                     jnp.where(lane < 64, pltpu.roll(v2, 96, 1), v1))
            for q in range(2):
                main[2 * index + q] = pairs[q]
                ex_out[2 * index + q] = pairs[q][8:24]
            halo = jnp.where(lane < 32, v2, jnp.where(lane < 64, v1, jnp.where(lane < 96, v0, v2)))
            half_f32[g * HR + j * S2:g * HR + (j + 1) * S2, :] = halo

    def halo_copy(g, k):
        return remote(halo_out.at[g], halo_in.at[k, g], halo_sem.at[16 * k + g], halo_sem.at[16 * k + 8 + g],
                      (after, cross_after)[k])

    def send_halo(g):
        halo_out[g] = half_f32[g * HR:(g + 1) * HR, :].astype(jnp.bfloat16)

        @pl.when(t < NTM - 1)
        def _():
            for k in range(2):
                halo_copy(g, k).start()

    lane8 = lax.broadcasted_iota(jnp.int32, (8, 128), 1)

    rows_of = [xs[d] * 48 for d in ORDER]

    def widen(g, j, q, first8, second8, base_s, core):
        for k in range(2):
            ry = 4 * j + ((0, 1), (3, 2))[q][k]
            row = rows_of[g % 4] + 24 * ((h + g // 4) % 2) + core * 3 + 6 * ys[ry // 3] + ry % 3
            mask = (lane8 < 64) if k == 0 else (lane8 >= 64)
            wide[pl.ds(base_s * STEP + row, 8, stride=STEP), :] = jnp.where(mask, second8, 0.0)
            wide[pl.ds(row, 8, stride=STEP), :] = jnp.where(mask, first8, 0.0)

    def exchange_copy(g):
        rows = pl.ds(g * 2 * NCH, 2 * NCH)
        return remote(ex_out.at[rows], ex_in.at[rows], ex_sem.at[g], ex_sem.at[8 + g], sibling)

    copies = {}

    def close(g):
        @pl.when(t > 0)
        def _():
            for k in range(2):
                halo_copy(g, k).wait_recv()

        copies[g].wait_recv()
        for k in range(2):
            halo = halo_in[k, g].astype(jnp.float32)
            for j in range(NCH):
                packed = halo[j * S2 + 8 * k:(j + 1) * S2]
                place = lane[8 * k:]
                by32, by64 = pltpu.roll(packed, 32, 1), pltpu.roll(packed, 64, 1)
                for q in range(2):
                    index = 2 * (g * NCH + j) + q
                    part = jnp.where(place < 64, by64, by32) if q == 0 else jnp.where(place < 64, by32, by64)
                    v = (main, ex_in)[k][index] + jnp.where(place % 64 < 32, part, 0.0)
                    if k == 0:
                        widen(g, j, q, v[0:8], v[16:24], 8, c)
                    else:
                        widen(g, j, q, v[0:8], v[8:16], 4, 1 - c)

    def unit(g):
        compute(g)
        send_halo(g)
        copies[g] = start(exchange_copy(g))

    round2(0)
    own_copy.wait()
    unit(0)
    for n in (0, 1):
        for i in range(RC):
            z_second[2 * i + n].wait_recv()
        base(1, n)
    round3(0)
    round4(0)
    unit(1)
    unit(2)
    round1(1)
    unit(3)
    close(0)
    close(1)
    round2(1)
    unit(4)
    close(2)
    flush(20)
    round3(1)
    close(3)
    flush(8)
    last(1, 1, 1)
    unit(5)
    last(1, 1, -1)
    unit(6)
    close(4)
    last(1, 1, 2)
    for oa in (-1, 1, 2):
        last(1, 0, oa)
    unit(7)
    for g in (5, 6, 7):
        close(g)

    both = lax.broadcasted_iota(jnp.int32, (TS, 128), 1) % TS == lax.broadcasted_iota(jnp.int32, (TS, 128), 0)
    both = jnp.where(both, 1.0, 0.0).astype(jnp.bfloat16)

    leaving = []
    for s in range(SH):
        block = wide[s * STEP:s * STEP + R, :].astype(jnp.bfloat16)
        result[s] = lax.dot_general(both, block, (((1,), (1,)), ((), ())), preferred_element_type=jnp.float32)
        copy = pltpu.make_async_copy(result.at[s], out_ref.at[s], out_sem.at[s])
        copy.start()
        leaving.append(copy)

    flush(0)
    for copy in leaving:
        copy.wait()

    @pl.when(t < NTM - 1)
    def _():
        for g in range(8):
            for k in range(2):
                halo_copy(g, k).wait_send()


def body(shot_window, receiver_data, apertures, taper_index, taper_table):
    gathered = jnp.transpose(receiver_data, (1, 0, 2))
    bf, f4 = jnp.bfloat16, jnp.float32
    dma = pltpu.SemaphoreType.DMA
    out = pl.pallas_call(
        kernel,
        out_shape=jax.ShapeDtypeStruct((SH, TS, R), f4),
        in_specs=[pl.BlockSpec(memory_space=pltpu.HBM)] * 5,
        out_specs=pl.BlockSpec(memory_space=pl.ANY),
        scratch_shapes=[
            pltpu.VMEM((2, NX, UR, ROWS, K), bf),
            pltpu.VMEM((2, RC, 32, K), bf),
            pltpu.VMEM((4, SH), jnp.int32),
            pltpu.VMEM((4, SH), jnp.int32),
            pltpu.SMEM((16,), f4),
            pltpu.VMEM((SH, LAG, K), bf),
            pltpu.VMEM((SH, LAG, K), bf),
            pltpu.VMEM((SH, LAG, K), bf),
            pltpu.VMEM((2, LAG * S2, 128), f4),
            pltpu.VMEM((LAG * SH, 2 * K), bf),
            pltpu.VMEM((NKB, 128), f4),
            pltpu.VMEM((LAG * SH, UR * WIN), f4),
            pltpu.VMEM((48, S2, 128), f4),
            pltpu.VMEM((8 * HR, 128), f4),
            pltpu.VMEM((8, HR, 128), bf),
            pltpu.VMEM((2, 8, HR, 128), bf),
            pltpu.VMEM((48, 16, 128), f4),
            pltpu.VMEM((48, 16, 128), f4),
            pltpu.VMEM((16 * STEP, 128), f4),
            pltpu.VMEM((SH, TS, R), f4),
            dma((NSEM,)), dma((NSEM,)), dma((4 * RC,)), dma((4 * RC,)), dma((2,)), dma((32,)), dma((16,)), dma((SH,)), dma((5,)),
        ],
        compiler_params=pltpu.CompilerParams(collective_id=0, has_side_effects=True,
                                             vmem_limit_bytes=60 * 1024 * 1024),
    )(gathered, shot_window, apertures.T, taper_index.T, taper_table)
    return jnp.transpose(out, (1, 0, 2)).astype(bf)


def solution(mesh):
    in_specs = (P("shot", None, None), P("tm", "shot", None), P("shot", None), P("shot", None), P())
    out_specs = P("tm", "shot", None)
    return jax.shard_map(body, mesh=mesh, in_specs=in_specs, out_specs=out_specs, check_vma=False)
```

```python
import jax
import jax.numpy as jnp
from jax import lax
from jax.experimental import pallas as pl
from jax.experimental.pallas import tpu as pltpu
from jax.sharding import PartitionSpec as P

MESH = pl.DeviceIdType.MESH
NX, NY, NH, NC, NTM = 4, 4, 2, 2, 8
NKB, LAG, K = 8, 32, 256
SH, RC, TS = 12, 3, 64
S2 = 2 * SH
UR = NY * RC
NCH = 3
R = 192
STEP = 200
HEAD, ROWS, WIN = 16, 112, 96
ORDER = (0, 1, 3, 2)
HR = 80
NSEM = 80

HALF = ((0, 32), (32, 32))
PLUS = ((16, 16), (32, 16))
MINUS = ((0, 16), (48, 16))


def device(x, y, h, c, t):
    return (((x * NH + h) * NY + y) * NC + c, t)


def kernel(x_ref, shot_hbm, aper_hbm, tidx_hbm, table_hbm, out_ref,
           xg, aper_ref, tidx_ref, table_ref, shot_ref, op_own, op_sib, op_f32, op_all, wt, prod, main, half_f32, halo_out, halo_in,
           ex_out, ex_in, wide, result, send_sem, recv_sem, z_send, z_recv, op_sem, halo_sem, ex_sem, out_sem, local_sem):
    shot_i = lax.axis_index("shot")
    t = lax.axis_index("tm")
    c = shot_i % 2
    y = (shot_i // 2) % 4
    h = (shot_i // 8) % 2
    x = shot_i // 16
    xs = [(x + d) % NX for d in range(NX)]
    ys = [(y + d) % NY for d in range(NY)]
    across = device(x, y, 1 - h, c, t)
    sibling = device(x, y, h, 1 - c, t)
    after = device(x, y, h, c, (t + 1) % NTM)
    before = device(x, y, h, c, (t + NTM - 1) % NTM)
    near = {
        ("x", 1): device((x + 1) % NX, y, h, c, t),
        ("x", -1): device((x + NX - 1) % NX, y, h, c, t),
        ("y", 1): device(x, (y + 1) % NY, h, c, t),
        ("y", -1): device(x, (y + NY - 1) % NY, h, c, t),
    }
    cross_after = device(x, y, h, 1 - c, (t + 1) % NTM)
    cross_before = device(x, y, h, 1 - c, (t + NTM - 1) % NTM)
    partners = list(near.values()) + [across, sibling, after, before, cross_after, cross_before]

    barrier = pltpu.get_barrier_semaphore()
    for who in partners:
        pl.semaphore_signal(barrier, inc=1, device_id=who, device_id_type=MESH)
    own_copy = pltpu.make_async_copy(x_ref, xg.at[0, 0, pl.ds(0, RC), pl.ds(HEAD, TS)], local_sem.at[0])
    own_copy.start()
    shot_copy = pltpu.make_async_copy(shot_hbm, shot_ref, local_sem.at[1])
    shot_copy.start()
    small = [pltpu.make_async_copy(a, b, local_sem.at[2 + i])
             for i, (a, b) in enumerate(((aper_hbm, aper_ref), (tidx_hbm, tidx_ref), (table_hbm, table_ref)))]
    for copy in small:
        copy.start()

    pl.semaphore_wait(barrier, len(partners))

    sends = []
    kinds = {}

    def slot(l, dx, dy, rows):
        return xg.at[l, dx % NX, pl.ds(RC * (dy % NY), RC), pl.ds(HEAD + rows[0], rows[1])]

    def remote(src, dst, ssem, rsem, who):
        return pltpu.make_async_remote_copy(src_ref=src, dst_ref=dst, send_sem=ssem, recv_sem=rsem,
                                            device_id=who, device_id_type=MESH)

    def start(copy):
        copy.start()
        sends.append(copy)
        return copy

    def flush(keep):
        while len(sends) > keep:
            sends.pop(0).wait_send()

    z_copies = [start(remote(x_ref.at[pl.ds(i, 1), pl.ds(32 * n, 32)], xg.at[1, 0, pl.ds(i, 1), pl.ds(HEAD + 32 * n, 32)],
                             z_send.at[n * RC + i], z_recv.at[n * RC + i], across))
                for n in range(2) for i in range(RC)]

    def send(l, n, oa, ob, rows, axis, way):
        first = "y" if n == 0 else "x"
        dx, dy = (ob, oa) if first == "y" else (oa, ob)
        step = way if axis == first else 0
        other = way if axis != first else 0
        key = (l, n, oa - step, ob - other, rows)
        k = kinds.setdefault(("sem",) + key + (axis, way), len([q for q in kinds if q[0] == "sem"]))
        src = slot(l, dx, dy, rows)
        if l == 0 and oa == 0 and ob == 0:
            src = x_ref.at[:, pl.ds(rows[0], rows[1])]
        back = (-way, 0) if axis == "x" else (0, -way)
        dst = slot(l, dx + back[0], dy + back[1], rows)
        kinds[key] = start(remote(src, dst, send_sem.at[k], recv_sem.at[k], near[(axis, way)]))

    def recv(l, n, oa, ob, rows):
        kinds[(l, n, oa, ob, rows)].wait_recv()

    def axes(n):
        return ("y", "x") if n == 0 else ("x", "y")

    def base(l, n):
        a, b = axes(n)
        for axis in (a, b):
            for way in (1, -1):
                send(l, n, 0, 0, HALF[n], axis, way)

    def round1(l):
        for n in (0, 1):
            a, b = axes(n)
            for off, way, piece in ((-1, 1, PLUS), (1, -1, MINUS)):
                recv(l, n, off, 0, HALF[n])
                send(l, n, off, 0, piece[n], a, way)
                for w in (1, -1):
                    send(l, n, off, 0, HALF[n], b, w)
        for n in (0, 1):
            a, b = axes(n)
            for off, way, piece in ((-1, 1, PLUS), (1, -1, MINUS)):
                recv(l, n, 0, off, HALF[n])
                send(l, n, 0, off, piece[n], b, way)

    def round2(l):
        for n in (0, 1):
            a, b = axes(n)
            recv(l, n, -2, 0, PLUS[n])
            recv(l, n, 2, 0, MINUS[n])
            for w in (1, -1):
                send(l, n, 2, 0, HALF[n], b, w)
        for oa in (-1, 1):
            for n in (0, 1):
                a, b = axes(n)
                for off, way, piece in ((-1, 1, PLUS), (1, -1, MINUS)):
                    recv(l, n, oa, off, HALF[n])
                    send(l, n, oa, off, piece[n], b, way)
        for n in (0, 1):
            recv(l, n, 0, -2, PLUS[n])
            recv(l, n, 0, 2, MINUS[n])

    def round3(l):
        for n in (0, 1):
            a, b = axes(n)
            for off, way, piece in ((-1, 1, PLUS), (1, -1, MINUS)):
                recv(l, n, 2, off, HALF[n])
                send(l, n, 2, off, piece[n], b, way)

    def last(l, n, oa):
        recv(l, n, oa, -2, PLUS[n])
        recv(l, n, oa, 2, MINUS[n])

    def round4(l):
        for oa in (-1, 1, 2):
            for n in (0, 1):
                last(l, n, oa)

    base(0, 0)
    base(0, 1)

    for copy in small:
        copy.wait()
    wt[...] = jnp.zeros_like(wt)
    tidx = tidx_ref[...]
    aper = aper_ref[...]
    picked = jnp.zeros(tidx.shape, jnp.float32)
    for j in range(16):
        picked = picked + jnp.where(tidx == j, table_ref[j], jnp.float32(0.0))
    for b in range(NKB):
        wt[b:b + 1, 0:SH] = jnp.sum(jnp.where(aper == b, picked, jnp.float32(0.0)), axis=0, keepdims=True)
    weight = wt[...].T
    block = lax.broadcasted_iota(jnp.int32, (16, K), 1) // (K // NKB)
    spread = jnp.zeros((16, K), jnp.float32)
    for b in range(NKB):
        spread = jnp.where(block == b, weight[0:16, b:b + 1], spread)
    shot_copy.wait()
    for s in range(SH):
        op_own[s] = (shot_ref[s].astype(jnp.float32) * spread[s:s + 1, :]).astype(jnp.bfloat16)
    op_copy = start(remote(op_own, op_sib, op_sem.at[0], op_sem.at[1], sibling))

    round1(0)
    for l in range(2):
        xg[l, :, :, 0:HEAD, :] = jnp.zeros((NX, UR, HEAD, K), jnp.bfloat16)
        xg[l, :, :, HEAD + TS:ROWS, :] = jnp.zeros((NX, UR, ROWS - HEAD - TS, K), jnp.bfloat16)
    half_f32[...] = jnp.zeros_like(half_f32)

    @pl.when(t == 0)
    def _():
        halo_in[...] = jnp.zeros_like(halo_in)

    def place(ref, s, row):
        v = ref[s].astype(jnp.float32)
        for q in range(2):
            op_f32[q, pl.ds(row, LAG, stride=S2), :] = v[:, q * 128:(q + 1) * 128]

    for s in range(SH):
        place(op_own, s, s if s < 8 else 8 + s)
    op_copy.wait_recv()
    for s in range(SH):
        place(op_sib, s, 8 + s if s < 8 else 12 + s)
    for q in range(2):
        for a in range(2):
            cols = a * K + q * 128
            op_all[:, cols:cols + 128] = op_f32[q, a * LAG * SH:(a + 1) * LAG * SH, :].astype(jnp.bfloat16)

    lane = lax.broadcasted_iota(jnp.int32, (S2, 128), 1)

    def compute(g):
        l, ux = g // 4, ORDER[g % 4]
        for r0, nr in ((0, 8), (8, 4)):
            late = xg[l, ux, r0:r0 + nr, HEAD:HEAD + WIN, :].reshape(nr * WIN, K)
            early = xg[l, ux, r0:r0 + nr, 0:WIN, :].reshape(nr * WIN, K)
            prod[:, r0 * WIN:(r0 + nr) * WIN] = lax.dot_general(
                op_all[...], jnp.concatenate([late, early], axis=1), (((1,), (1,)), ((), ())),
                preferred_element_type=jnp.float32)
        for j in range(NCH):
            acc = prod[0:S2, j * 4 * WIN:(j + 1) * 4 * WIN]
            for b in range(1, LAG // 2):
                acc = acc + pltpu.roll(prod[b * S2:(b + 1) * S2, j * 4 * WIN:(j + 1) * 4 * WIN], b, 1)
            v0, v1, v2 = acc[:, 0:128], acc[:, 128:256], acc[:, 256:384]
            index = g * NCH + j
            pairs = (jnp.where(lane < 64, v0, pltpu.roll(jnp.where(lane >= 96, v0, v1), 96, 1)),
                     jnp.where(lane < 64, pltpu.roll(v2, 96, 1), v1))
            for q in range(2):
                main[2 * index + q] = pairs[q]
                ex_out[2 * index + q] = pairs[q][8:24]
            halo = jnp.where(lane < 32, v2, jnp.where(lane < 64, v1, jnp.where(lane < 96, v0, v2)))
            half_f32[g * HR + j * S2:g * HR + (j + 1) * S2, :] = halo

    def halo_copy(g, k):
        return remote(halo_out.at[g], halo_in.at[k, g], halo_sem.at[16 * k + g], halo_sem.at[16 * k + 8 + g],
                      (after, cross_after)[k])

    def send_halo(g):
        halo_out[g] = half_f32[g * HR:(g + 1) * HR, :].astype(jnp.bfloat16)

        @pl.when(t < NTM - 1)
        def _():
            for k in range(2):
                halo_copy(g, k).start()

    lane8 = lax.broadcasted_iota(jnp.int32, (8, 128), 1)

    rows_of = [xs[d] * 48 for d in ORDER]

    def widen(g, j, q, first8, second8, base_s, core):
        for k in range(2):
            ry = 4 * j + ((0, 1), (3, 2))[q][k]
            row = rows_of[g % 4] + 24 * ((h + g // 4) % 2) + core * 3 + 6 * ys[ry // 3] + ry % 3
            mask = (lane8 < 64) if k == 0 else (lane8 >= 64)
            wide[pl.ds(base_s * STEP + row, 8, stride=STEP), :] = jnp.where(mask, second8, 0.0)
            wide[pl.ds(row, 8, stride=STEP), :] = jnp.where(mask, first8, 0.0)

    def exchange_copy(g):
        rows = pl.ds(g * 2 * NCH, 2 * NCH)
        return remote(ex_out.at[rows], ex_in.at[rows], ex_sem.at[g], ex_sem.at[8 + g], sibling)

    copies = {}

    def close(g):
        @pl.when(t > 0)
        def _():
            for k in range(2):
                halo_copy(g, k).wait_recv()

        copies[g].wait_recv()
        for k in range(2):
            halo = halo_in[k, g].astype(jnp.float32)
            for j in range(NCH):
                packed = halo[j * S2 + 8 * k:(j + 1) * S2]
                place = lane[8 * k:]
                by32, by64 = pltpu.roll(packed, 32, 1), pltpu.roll(packed, 64, 1)
                for q in range(2):
                    index = 2 * (g * NCH + j) + q
                    part = jnp.where(place < 64, by64, by32) if q == 0 else jnp.where(place < 64, by32, by64)
                    v = (main, ex_in)[k][index] + jnp.where(place % 64 < 32, part, 0.0)
                    if k == 0:
                        widen(g, j, q, v[0:8], v[16:24], 8, c)
                    else:
                        widen(g, j, q, v[0:8], v[8:16], 4, 1 - c)

    def unit(g):
        compute(g)
        send_halo(g)
        copies[g] = start(exchange_copy(g))

    round2(0)
    own_copy.wait()
    unit(0)
    round3(0)
    for n in (0, 1):
        for i in range(RC):
            z_copies[n * RC + i].wait_recv()
        base(1, n)
    round4(0)
    unit(1)
    unit(2)
    round1(1)
    unit(3)
    close(0)
    close(1)
    round2(1)
    unit(4)
    close(2)
    flush(20)
    round3(1)
    close(3)
    flush(8)
    last(1, 1, 1)
    unit(5)
    last(1, 1, -1)
    unit(6)
    close(4)
    close(5)
    last(1, 1, 2)
    for oa in (-1, 1, 2):
        last(1, 0, oa)
    unit(7)
    for g in (6, 7):
        close(g)

    both = lax.broadcasted_iota(jnp.int32, (TS, 128), 1) % TS == lax.broadcasted_iota(jnp.int32, (TS, 128), 0)
    both = jnp.where(both, 1.0, 0.0).astype(jnp.bfloat16)

    leaving = []
    for s in range(SH):
        block = wide[s * STEP:s * STEP + R, :].astype(jnp.bfloat16)
        result[s] = lax.dot_general(both, block, (((1,), (1,)), ((), ())),
                                    preferred_element_type=jnp.float32).astype(jnp.bfloat16)
        copy = pltpu.make_async_copy(result.at[s], out_ref.at[s], out_sem.at[s])
        copy.start()
        leaving.append(copy)

    flush(0)
    for copy in leaving:
        copy.wait()

    @pl.when(t < NTM - 1)
    def _():
        for g in range(8):
            for k in range(2):
                halo_copy(g, k).wait_send()


def body(shot_window, receiver_data, apertures, taper_index, taper_table):
    gathered = jnp.transpose(receiver_data, (1, 0, 2))
    bf, f4 = jnp.bfloat16, jnp.float32
    dma = pltpu.SemaphoreType.DMA
    out = pl.pallas_call(
        kernel,
        out_shape=jax.ShapeDtypeStruct((SH, TS, R), bf),
        in_specs=[pl.BlockSpec(memory_space=pltpu.HBM)] * 5,
        out_specs=pl.BlockSpec(memory_space=pl.ANY),
        scratch_shapes=[
            pltpu.VMEM((2, NX, UR, ROWS, K), bf),
            pltpu.VMEM((4, SH), jnp.int32),
            pltpu.VMEM((4, SH), jnp.int32),
            pltpu.SMEM((16,), f4),
            pltpu.VMEM((SH, LAG, K), bf),
            pltpu.VMEM((SH, LAG, K), bf),
            pltpu.VMEM((SH, LAG, K), bf),
            pltpu.VMEM((2, LAG * S2, 128), f4),
            pltpu.VMEM((LAG * SH, 2 * K), bf),
            pltpu.VMEM((NKB, 128), f4),
            pltpu.VMEM((LAG * SH, UR * WIN), f4),
            pltpu.VMEM((48, S2, 128), f4),
            pltpu.VMEM((8 * HR, 128), f4),
            pltpu.VMEM((8, HR, 128), bf),
            pltpu.VMEM((2, 8, HR, 128), bf),
            pltpu.VMEM((48, 16, 128), f4),
            pltpu.VMEM((48, 16, 128), f4),
            pltpu.VMEM((16 * STEP, 128), f4),
            pltpu.VMEM((SH, TS, R), bf),
            dma((NSEM,)), dma((NSEM,)), dma((2 * RC,)), dma((2 * RC,)), dma((2,)), dma((32,)), dma((16,)), dma((SH,)), dma((5,)),
        ],
        compiler_params=pltpu.CompilerParams(collective_id=0, has_side_effects=True,
                                             vmem_limit_bytes=60 * 1024 * 1024),
    )(gathered, shot_window, apertures.T, taper_index.T, taper_table)
    return jnp.transpose(out, (1, 0, 2))


def solution(mesh):
    in_specs = (P("shot", None, None), P("tm", "shot", None), P("shot", None), P("shot", None), P())
    out_specs = P("tm", "shot", None)
    return jax.shard_map(body, mesh=mesh, in_specs=in_specs, out_specs=out_specs, check_vma=False)
```

```python
import jax
import jax.numpy as jnp
from jax import lax
from jax.experimental import pallas as pl
from jax.experimental.pallas import tpu as pltpu
from jax.sharding import PartitionSpec as P

MESH = pl.DeviceIdType.MESH
NX, NY, NH, NC, NTM = 4, 4, 2, 2, 8
NZ = NH * NTM
NKB, LAG, K = 8, 32, 256
SH, RC, TS = 12, 3, 64
S2 = 2 * SH
UR = NY * RC
NCH = 3
R = 192
STEP = 200
HEAD, ROWS, WIN = 16, 112, 96
ORDER = (0, 1, 3, 2)
HR = 80
NSEM = 80

HALF = ((0, 32), (32, 32))
PLUS = ((16, 16), (32, 16))
MINUS = ((0, 16), (48, 16))


def device(x, y, h, c, t):
    return (((x * NH + h) * NY + y) * NC + c, t)


def kernel(x_ref, shot_hbm, aper_hbm, tidx_hbm, table_hbm, out_ref,
           xg, rz, aper_ref, tidx_ref, table_ref, shot_ref, op_own, op_sib, op_f32, op_all, wt, prod, main, half_f32, halo_out, halo_in,
           ex_out, ex_in, wide, result, send_sem, recv_sem, z_send, z_recv, op_sem, halo_sem, ex_sem, out_sem, local_sem):
    shot_i = lax.axis_index("shot")
    t = lax.axis_index("tm")
    c = shot_i % 2
    y = (shot_i // 2) % 4
    h = (shot_i // 8) % 2
    x = shot_i // 16
    z = h * NTM + t
    xs = [(x + d) % NX for d in range(NX)]
    ys = [(y + d) % NY for d in range(NY)]
    zp = (z + 4) % NZ
    zm = (z + NZ - 4) % NZ
    up = device(x, y, zp // NTM, c, zp % NTM)
    down = device(x, y, zm // NTM, c, zm % NTM)
    sibling = device(x, y, h, 1 - c, t)
    after = device(x, y, h, c, (t + 1) % NTM)
    before = device(x, y, h, c, (t + NTM - 1) % NTM)
    near = {
        ("x", 1): device((x + 1) % NX, y, h, c, t),
        ("x", -1): device((x + NX - 1) % NX, y, h, c, t),
        ("y", 1): device(x, (y + 1) % NY, h, c, t),
        ("y", -1): device(x, (y + NY - 1) % NY, h, c, t),
    }
    cross_after = device(x, y, h, 1 - c, (t + 1) % NTM)
    cross_before = device(x, y, h, 1 - c, (t + NTM - 1) % NTM)
    partners = list(near.values()) + [up, down, sibling, after, before, cross_after, cross_before]

    barrier = pltpu.get_barrier_semaphore()
    for who in partners:
        pl.semaphore_signal(barrier, inc=1, device_id=who, device_id_type=MESH)
    own_copy = pltpu.make_async_copy(x_ref, xg.at[0, 0, pl.ds(0, RC), pl.ds(HEAD, TS)], local_sem.at[0])
    own_copy.start()
    shot_copy = pltpu.make_async_copy(shot_hbm, shot_ref, local_sem.at[1])
    shot_copy.start()
    small = [pltpu.make_async_copy(a, b, local_sem.at[2 + i])
             for i, (a, b) in enumerate(((aper_hbm, aper_ref), (tidx_hbm, tidx_ref), (table_hbm, table_ref)))]
    for copy in small:
        copy.start()

    pl.semaphore_wait(barrier, len(partners))

    sends = []
    kinds = {}

    def slot(l, dx, dy, rows):
        return xg.at[l, dx % NX, pl.ds(RC * (dy % NY), RC), pl.ds(HEAD + rows[0], rows[1])]

    def remote(src, dst, ssem, rsem, who):
        return pltpu.make_async_remote_copy(src_ref=src, dst_ref=dst, send_sem=ssem, recv_sem=rsem,
                                            device_id=who, device_id_type=MESH)

    def start(copy):
        copy.start()
        sends.append(copy)
        return copy

    def flush(keep):
        while len(sends) > keep:
            sends.pop(0).wait_send()

    z_first = [[start(remote(x_ref.at[pl.ds(i, 1), pl.ds(32 * d, 32)], rz.at[d, pl.ds(i, 1)],
                             z_send.at[2 * i + d], z_recv.at[2 * i + d], who))
                for d, who in ((0, up), (1, down))] for i in range(RC)]

    def send(l, n, oa, ob, rows, axis, way):
        first = "y" if n == 0 else "x"
        dx, dy = (ob, oa) if first == "y" else (oa, ob)
        step = way if axis == first else 0
        other = way if axis != first else 0
        key = (l, n, oa - step, ob - other, rows)
        k = kinds.setdefault(("sem",) + key + (axis, way), len([q for q in kinds if q[0] == "sem"]))
        src = slot(l, dx, dy, rows)
        if l == 0 and oa == 0 and ob == 0:
            src = x_ref.at[:, pl.ds(rows[0], rows[1])]
        back = (-way, 0) if axis == "x" else (0, -way)
        dst = slot(l, dx + back[0], dy + back[1], rows)
        kinds[key] = start(remote(src, dst, send_sem.at[k], recv_sem.at[k], near[(axis, way)]))

    def recv(l, n, oa, ob, rows):
        kinds[(l, n, oa, ob, rows)].wait_recv()

    def axes(n):
        return ("y", "x") if n == 0 else ("x", "y")

    def base(l, n):
        a, b = axes(n)
        for axis in (a, b):
            for way in (1, -1):
                send(l, n, 0, 0, HALF[n], axis, way)

    def round1(l):
        for n in (0, 1):
            a, b = axes(n)
            for off, way, piece in ((-1, 1, PLUS), (1, -1, MINUS)):
                recv(l, n, off, 0, HALF[n])
                send(l, n, off, 0, piece[n], a, way)
                for w in (1, -1):
                    send(l, n, off, 0, HALF[n], b, w)
        for n in (0, 1):
            a, b = axes(n)
            for off, way, piece in ((-1, 1, PLUS), (1, -1, MINUS)):
                recv(l, n, 0, off, HALF[n])
                send(l, n, 0, off, piece[n], b, way)

    def round2(l):
        for n in (0, 1):
            a, b = axes(n)
            recv(l, n, -2, 0, PLUS[n])
            recv(l, n, 2, 0, MINUS[n])
            for w in (1, -1):
                send(l, n, 2, 0, HALF[n], b, w)
        for oa in (-1, 1):
            for n in (0, 1):
                a, b = axes(n)
                for off, way, piece in ((-1, 1, PLUS), (1, -1, MINUS)):
                    recv(l, n, oa, off, HALF[n])
                    send(l, n, oa, off, piece[n], b, way)
        for n in (0, 1):
            recv(l, n, 0, -2, PLUS[n])
            recv(l, n, 0, 2, MINUS[n])

    def round3(l):
        for n in (0, 1):
            a, b = axes(n)
            for off, way, piece in ((-1, 1, PLUS), (1, -1, MINUS)):
                recv(l, n, 2, off, HALF[n])
                send(l, n, 2, off, piece[n], b, way)

    def last(l, n, oa):
        recv(l, n, oa, -2, PLUS[n])
        recv(l, n, oa, 2, MINUS[n])

    def round4(l):
        for oa in (-1, 1, 2):
            for n in (0, 1):
                last(l, n, oa)

    base(0, 0)
    base(0, 1)

    for copy in small:
        copy.wait()
    wt[...] = jnp.zeros_like(wt)
    tidx = tidx_ref[...]
    aper = aper_ref[...]
    picked = jnp.zeros(tidx.shape, jnp.float32)
    for j in range(16):
        picked = picked + jnp.where(tidx == j, table_ref[j], jnp.float32(0.0))
    for b in range(NKB):
        wt[b:b + 1, 0:SH] = jnp.sum(jnp.where(aper == b, picked, jnp.float32(0.0)), axis=0, keepdims=True)
    weight = wt[...].T
    block = lax.broadcasted_iota(jnp.int32, (16, K), 1) // (K // NKB)
    spread = jnp.zeros((16, K), jnp.float32)
    for b in range(NKB):
        spread = jnp.where(block == b, weight[0:16, b:b + 1], spread)
    shot_copy.wait()
    for s in range(SH):
        op_own[s] = (shot_ref[s].astype(jnp.float32) * spread[s:s + 1, :]).astype(jnp.bfloat16)
    op_copy = start(remote(op_own, op_sib, op_sem.at[0], op_sem.at[1], sibling))

    round1(0)
    for l in range(2):
        xg[l, :, :, 0:HEAD, :] = jnp.zeros((NX, UR, HEAD, K), jnp.bfloat16)
        xg[l, :, :, HEAD + TS:ROWS, :] = jnp.zeros((NX, UR, ROWS - HEAD - TS, K), jnp.bfloat16)
    half_f32[...] = jnp.zeros_like(half_f32)

    @pl.when(t == 0)
    def _():
        halo_in[...] = jnp.zeros_like(halo_in)

    z_second = []
    for i in range(RC):
        for d, who in ((0, up), (1, down)):
            z_first[i][d].wait_recv()
            dst = xg.at[1, 0, pl.ds(i, 1), pl.ds(HEAD + HALF[d][0], 32)]
            k = 2 * (RC + i) + d
            z_second.append(start(remote(rz.at[d, pl.ds(i, 1)], dst, z_send.at[k], z_recv.at[k], who)))

    def place(ref, s, row):
        v = ref[s].astype(jnp.float32)
        for q in range(2):
            op_f32[q, pl.ds(row, LAG, stride=S2), :] = v[:, q * 128:(q + 1) * 128]

    for s in range(SH):
        place(op_own, s, s if s < 8 else 8 + s)
    op_copy.wait_recv()
    for s in range(SH):
        place(op_sib, s, 8 + s if s < 8 else 12 + s)
    for q in range(2):
        for a in range(2):
            cols = a * K + q * 128
            op_all[:, cols:cols + 128] = op_f32[q, a * LAG * SH:(a + 1) * LAG * SH, :].astype(jnp.bfloat16)

    lane = lax.broadcasted_iota(jnp.int32, (S2, 128), 1)

    def compute(g):
        l, ux = g // 4, ORDER[g % 4]
        for r0, nr in ((0, 8), (8, 4)):
            late = xg[l, ux, r0:r0 + nr, HEAD:HEAD + WIN, :].reshape(nr * WIN, K)
            early = xg[l, ux, r0:r0 + nr, 0:WIN, :].reshape(nr * WIN, K)
            prod[:, r0 * WIN:(r0 + nr) * WIN] = lax.dot_general(
                op_all[...], jnp.concatenate([late, early], axis=1), (((1,), (1,)), ((), ())),
                preferred_element_type=jnp.float32)
        for j in range(NCH):
            acc = prod[0:S2, j * 4 * WIN:(j + 1) * 4 * WIN]
            for b in range(1, LAG // 2):
                acc = acc + pltpu.roll(prod[b * S2:(b + 1) * S2, j * 4 * WIN:(j + 1) * 4 * WIN], b, 1)
            v0, v1, v2 = acc[:, 0:128], acc[:, 128:256], acc[:, 256:384]
            index = g * NCH + j
            pairs = (jnp.where(lane < 64, v0, pltpu.roll(jnp.where(lane >= 96, v0, v1), 96, 1)),
                     jnp.where(lane < 64, pltpu.roll(v2, 96, 1), v1))
            for q in range(2):
                main[2 * index + q] = pairs[q]
                ex_out[2 * index + q] = pairs[q][8:24]
            halo = jnp.where(lane < 32, v2, jnp.where(lane < 64, v1, jnp.where(lane < 96, v0, v2)))
            half_f32[g * HR + j * S2:g * HR + (j + 1) * S2, :] = halo

    def halo_copy(g, k):
        return remote(halo_out.at[g], halo_in.at[k, g], halo_sem.at[16 * k + g], halo_sem.at[16 * k + 8 + g],
                      (after, cross_after)[k])

    def send_halo(g):
        halo_out[g] = half_f32[g * HR:(g + 1) * HR, :].astype(jnp.bfloat16)

        @pl.when(t < NTM - 1)
        def _():
            for k in range(2):
                halo_copy(g, k).start()

    lane8 = lax.broadcasted_iota(jnp.int32, (8, 128), 1)

    rows_of = [xs[d] * 48 for d in ORDER]

    def widen(g, j, q, first8, second8, base_s, core):
        for k in range(2):
            ry = 4 * j + ((0, 1), (3, 2))[q][k]
            row = rows_of[g % 4] + 24 * ((h + g // 4) % 2) + core * 3 + 6 * ys[ry // 3] + ry % 3
            mask = (lane8 < 64) if k == 0 else (lane8 >= 64)
            wide[pl.ds(base_s * STEP + row, 8, stride=STEP), :] = jnp.where(mask, second8, 0.0)
            wide[pl.ds(row, 8, stride=STEP), :] = jnp.where(mask, first8, 0.0)

    def exchange_copy(g):
        rows = pl.ds(g * 2 * NCH, 2 * NCH)
        return remote(ex_out.at[rows], ex_in.at[rows], ex_sem.at[g], ex_sem.at[8 + g], sibling)

    copies = {}

    def close(g):
        @pl.when(t > 0)
        def _():
            for k in range(2):
                halo_copy(g, k).wait_recv()

        copies[g].wait_recv()
        for k in range(2):
            halo = halo_in[k, g].astype(jnp.float32)
            for j in range(NCH):
                packed = halo[j * S2 + 8 * k:(j + 1) * S2]
                place = lane[8 * k:]
                by32, by64 = pltpu.roll(packed, 32, 1), pltpu.roll(packed, 64, 1)
                for q in range(2):
                    index = 2 * (g * NCH + j) + q
                    part = jnp.where(place < 64, by64, by32) if q == 0 else jnp.where(place < 64, by32, by64)
                    v = (main, ex_in)[k][index] + jnp.where(place % 64 < 32, part, 0.0)
                    if k == 0:
                        widen(g, j, q, v[0:8], v[16:24], 8, c)
                    else:
                        widen(g, j, q, v[0:8], v[8:16], 4, 1 - c)

    def unit(g):
        compute(g)
        send_halo(g)
        copies[g] = start(exchange_copy(g))

    round2(0)
    own_copy.wait()
    unit(0)
    round3(0)
    for n in (0, 1):
        for i in range(RC):
            z_second[2 * i + n].wait_recv()
        base(1, n)
    round4(0)
    unit(1)
    unit(2)
    round1(1)
    unit(3)
    close(0)
    close(1)
    round2(1)
    unit(4)
    close(2)
    flush(20)
    round3(1)
    close(3)
    flush(8)
    last(1, 1, 1)
    unit(5)
    last(1, 1, -1)
    unit(6)
    close(4)
    last(1, 1, 2)
    for oa in (-1, 1, 2):
        last(1, 0, oa)
    unit(7)
    for g in (5, 6, 7):
        close(g)

    both = lax.broadcasted_iota(jnp.int32, (TS, 128), 1) % TS == lax.broadcasted_iota(jnp.int32, (TS, 128), 0)
    both = jnp.where(both, 1.0, 0.0).astype(jnp.bfloat16)

    leaving = []
    for s in range(SH):
        block = wide[s * STEP:s * STEP + R, :].astype(jnp.bfloat16)
        result[s] = lax.dot_general(both, block, (((1,), (1,)), ((), ())),
                                    preferred_element_type=jnp.float32).astype(jnp.bfloat16)
        copy = pltpu.make_async_copy(result.at[s], out_ref.at[s], out_sem.at[s])
        copy.start()
        leaving.append(copy)

    flush(0)
    for copy in leaving:
        copy.wait()

    @pl.when(t < NTM - 1)
    def _():
        for g in range(8):
            for k in range(2):
                halo_copy(g, k).wait_send()


def body(shot_window, receiver_data, apertures, taper_index, taper_table):
    gathered = jnp.transpose(receiver_data, (1, 0, 2))
    bf, f4 = jnp.bfloat16, jnp.float32
    dma = pltpu.SemaphoreType.DMA
    out = pl.pallas_call(
        kernel,
        out_shape=jax.ShapeDtypeStruct((SH, TS, R), bf),
        in_specs=[pl.BlockSpec(memory_space=pltpu.HBM)] * 5,
        out_specs=pl.BlockSpec(memory_space=pl.ANY),
        scratch_shapes=[
            pltpu.VMEM((2, NX, UR, ROWS, K), bf),
            pltpu.VMEM((2, RC, 32, K), bf),
            pltpu.VMEM((4, SH), jnp.int32),
            pltpu.VMEM((4, SH), jnp.int32),
            pltpu.SMEM((16,), f4),
            pltpu.VMEM((SH, LAG, K), bf),
            pltpu.VMEM((SH, LAG, K), bf),
            pltpu.VMEM((SH, LAG, K), bf),
            pltpu.VMEM((2, LAG * S2, 128), f4),
            pltpu.VMEM((LAG * SH, 2 * K), bf),
            pltpu.VMEM((NKB, 128), f4),
            pltpu.VMEM((LAG * SH, UR * WIN), f4),
            pltpu.VMEM((48, S2, 128), f4),
            pltpu.VMEM((8 * HR, 128), f4),
            pltpu.VMEM((8, HR, 128), bf),
            pltpu.VMEM((2, 8, HR, 128), bf),
            pltpu.VMEM((48, 16, 128), f4),
            pltpu.VMEM((48, 16, 128), f4),
            pltpu.VMEM((16 * STEP, 128), f4),
            pltpu.VMEM((SH, TS, R), bf),
            dma((NSEM,)), dma((NSEM,)), dma((4 * RC,)), dma((4 * RC,)), dma((2,)), dma((32,)), dma((16,)), dma((SH,)), dma((5,)),
        ],
        compiler_params=pltpu.CompilerParams(collective_id=0, has_side_effects=True,
                                             vmem_limit_bytes=60 * 1024 * 1024),
    )(gathered, shot_window, apertures.T, taper_index.T, taper_table)
    return jnp.transpose(out, (1, 0, 2))


def solution(mesh):
    in_specs = (P("shot", None, None), P("tm", "shot", None), P("shot", None), P("shot", None), P())
    out_specs = P("tm", "shot", None)
    return jax.shard_map(body, mesh=mesh, in_specs=in_specs, out_specs=out_specs, check_vma=False)
```

```python
import jax
import jax.numpy as jnp
from jax import lax
from jax.experimental import pallas as pl
from jax.experimental.pallas import tpu as pltpu
from jax.sharding import PartitionSpec as P

MESH = pl.DeviceIdType.MESH
NX, NY, NH, NC, NTM = 4, 4, 2, 2, 8
NZ = NH * NTM
NKB, LAG, K = 8, 32, 256
SH, RC, TS = 12, 3, 64
S2 = 2 * SH
UR = NY * RC
NCH = 3
R = 192
STEP = 200
HEAD, ROWS, WIN = 16, 112, 96
ORDER = (0, 1, 3, 2)
HR = 80
NSEM = 80

HALF = ((0, 32), (32, 32))
PLUS = ((16, 16), (32, 16))
MINUS = ((0, 16), (48, 16))


def device(x, y, h, c, t):
    return (((x * NH + h) * NY + y) * NC + c, t)


def kernel(x_ref, shot_hbm, aper_hbm, tidx_hbm, table_hbm, out_ref,
           xg, rz, aper_ref, tidx_ref, table_ref, shot_ref, op_own, op_sib, op_f32, op_all, wt, prod, main, half_f32, halo_out, halo_in,
           ex_out, ex_in, wide, result, send_sem, recv_sem, z_send, z_recv, op_sem, halo_sem, ex_sem, out_sem, local_sem):
    shot_i = lax.axis_index("shot")
    t = lax.axis_index("tm")
    c = shot_i % 2
    y = (shot_i // 2) % 4
    h = (shot_i // 8) % 2
    x = shot_i // 16
    z = h * NTM + t
    xs = [(x + d) % NX for d in range(NX)]
    ys = [(y + d) % NY for d in range(NY)]
    zp = (z + 4) % NZ
    zm = (z + NZ - 4) % NZ
    up = device(x, y, zp // NTM, c, zp % NTM)
    down = device(x, y, zm // NTM, c, zm % NTM)
    sibling = device(x, y, h, 1 - c, t)
    after = device(x, y, h, c, (t + 1) % NTM)
    before = device(x, y, h, c, (t + NTM - 1) % NTM)
    near = {
        ("x", 1): device((x + 1) % NX, y, h, c, t),
        ("x", -1): device((x + NX - 1) % NX, y, h, c, t),
        ("y", 1): device(x, (y + 1) % NY, h, c, t),
        ("y", -1): device(x, (y + NY - 1) % NY, h, c, t),
    }
    cross_after = device(x, y, h, 1 - c, (t + 1) % NTM)
    cross_before = device(x, y, h, 1 - c, (t + NTM - 1) % NTM)
    partners = list(near.values()) + [up, down, sibling, after, before, cross_after, cross_before]

    barrier = pltpu.get_barrier_semaphore()
    for who in partners:
        pl.semaphore_signal(barrier, inc=1, device_id=who, device_id_type=MESH)
    own_copy = pltpu.make_async_copy(x_ref, xg.at[0, 0, pl.ds(0, RC), pl.ds(HEAD, TS)], local_sem.at[0])
    own_copy.start()
    shot_copy = pltpu.make_async_copy(shot_hbm, shot_ref, local_sem.at[1])
    shot_copy.start()
    small = [pltpu.make_async_copy(a, b, local_sem.at[2 + i])
             for i, (a, b) in enumerate(((aper_hbm, aper_ref), (tidx_hbm, tidx_ref), (table_hbm, table_ref)))]
    for copy in small:
        copy.start()

    pl.semaphore_wait(barrier, len(partners))

    sends = []
    kinds = {}

    def slot(l, dx, dy, rows):
        return xg.at[l, dx % NX, pl.ds(RC * (dy % NY), RC), pl.ds(HEAD + rows[0], rows[1])]

    def remote(src, dst, ssem, rsem, who):
        return pltpu.make_async_remote_copy(src_ref=src, dst_ref=dst, send_sem=ssem, recv_sem=rsem,
                                            device_id=who, device_id_type=MESH)

    def start(copy):
        copy.start()
        sends.append(copy)
        return copy

    def flush(keep):
        while len(sends) > keep:
            sends.pop(0).wait_send()

    z_first = [[start(remote(x_ref.at[pl.ds(i, 1), pl.ds(32 * d, 32)], rz.at[d, pl.ds(i, 1)],
                             z_send.at[2 * i + d], z_recv.at[2 * i + d], who))
                for d, who in ((0, up), (1, down))] for i in range(RC)]

    def send(l, n, oa, ob, rows, axis, way):
        first = "y" if n == 0 else "x"
        dx, dy = (ob, oa) if first == "y" else (oa, ob)
        step = way if axis == first else 0
        other = way if axis != first else 0
        key = (l, n, oa - step, ob - other, rows)
        k = kinds.setdefault(("sem",) + key + (axis, way), len([q for q in kinds if q[0] == "sem"]))
        src = slot(l, dx, dy, rows)
        if l == 0 and oa == 0 and ob == 0:
            src = x_ref.at[:, pl.ds(rows[0], rows[1])]
        back = (-way, 0) if axis == "x" else (0, -way)
        dst = slot(l, dx + back[0], dy + back[1], rows)
        kinds[key] = start(remote(src, dst, send_sem.at[k], recv_sem.at[k], near[(axis, way)]))

    def recv(l, n, oa, ob, rows):
        kinds[(l, n, oa, ob, rows)].wait_recv()

    def axes(n):
        return ("y", "x") if n == 0 else ("x", "y")

    def base(l, n):
        a, b = axes(n)
        for axis in (a, b):
            for way in (1, -1):
                send(l, n, 0, 0, HALF[n], axis, way)

    def round1(l):
        for n in (0, 1):
            a, b = axes(n)
            for off, way, piece in ((-1, 1, PLUS), (1, -1, MINUS)):
                recv(l, n, off, 0, HALF[n])
                send(l, n, off, 0, piece[n], a, way)
                for w in (1, -1):
                    send(l, n, off, 0, HALF[n], b, w)
        for n in (0, 1):
            a, b = axes(n)
            for off, way, piece in ((-1, 1, PLUS), (1, -1, MINUS)):
                recv(l, n, 0, off, HALF[n])
                send(l, n, 0, off, piece[n], b, way)

    def round2(l):
        for n in (0, 1):
            a, b = axes(n)
            recv(l, n, -2, 0, PLUS[n])
            recv(l, n, 2, 0, MINUS[n])
            for w in (1, -1):
                send(l, n, 2, 0, HALF[n], b, w)
        for oa in (-1, 1):
            for n in (0, 1):
                a, b = axes(n)
                for off, way, piece in ((-1, 1, PLUS), (1, -1, MINUS)):
                    recv(l, n, oa, off, HALF[n])
                    send(l, n, oa, off, piece[n], b, way)
        for n in (0, 1):
            recv(l, n, 0, -2, PLUS[n])
            recv(l, n, 0, 2, MINUS[n])

    def round3(l):
        for n in (0, 1):
            a, b = axes(n)
            for off, way, piece in ((-1, 1, PLUS), (1, -1, MINUS)):
                recv(l, n, 2, off, HALF[n])
                send(l, n, 2, off, piece[n], b, way)

    def last(l, n, oa):
        recv(l, n, oa, -2, PLUS[n])
        recv(l, n, oa, 2, MINUS[n])

    def round4(l):
        for oa in (-1, 1, 2):
            for n in (0, 1):
                last(l, n, oa)

    base(0, 0)
    base(0, 1)

    for copy in small:
        copy.wait()
    wt[...] = jnp.zeros_like(wt)
    tidx = tidx_ref[...]
    aper = aper_ref[...]
    picked = jnp.zeros(tidx.shape, jnp.float32)
    for j in range(16):
        picked = picked + jnp.where(tidx == j, table_ref[j], jnp.float32(0.0))
    for b in range(NKB):
        wt[b:b + 1, 0:SH] = jnp.sum(jnp.where(aper == b, picked, jnp.float32(0.0)), axis=0, keepdims=True)
    weight = wt[...].T
    block = lax.broadcasted_iota(jnp.int32, (16, K), 1) // (K // NKB)
    spread = jnp.zeros((16, K), jnp.float32)
    for b in range(NKB):
        spread = jnp.where(block == b, weight[0:16, b:b + 1], spread)
    shot_copy.wait()
    for s in range(SH):
        op_own[s] = (shot_ref[s].astype(jnp.float32) * spread[s:s + 1, :]).astype(jnp.bfloat16)
    op_copy = start(remote(op_own, op_sib, op_sem.at[0], op_sem.at[1], sibling))

    round1(0)
    for l in range(2):
        xg[l, :, :, 0:HEAD, :] = jnp.zeros((NX, UR, HEAD, K), jnp.bfloat16)
        xg[l, :, :, HEAD + TS:ROWS, :] = jnp.zeros((NX, UR, ROWS - HEAD - TS, K), jnp.bfloat16)
    half_f32[...] = jnp.zeros_like(half_f32)

    @pl.when(t == 0)
    def _():
        halo_in[...] = jnp.zeros_like(halo_in)

    def place(ref, s, row):
        v = ref[s].astype(jnp.float32)
        for q in range(2):
            op_f32[q, pl.ds(row, LAG, stride=S2), :] = v[:, q * 128:(q + 1) * 128]

    for s in range(SH):
        place(op_own, s, s if s < 8 else 8 + s)
    op_copy.wait_recv()
    for s in range(SH):
        place(op_sib, s, 8 + s if s < 8 else 12 + s)
    for q in range(2):
        for a in range(2):
            cols = a * K + q * 128
            op_all[:, cols:cols + 128] = op_f32[q, a * LAG * SH:(a + 1) * LAG * SH, :].astype(jnp.bfloat16)

    z_second = []
    for i in range(RC):
        for d, who in ((0, up), (1, down)):
            z_first[i][d].wait_recv()
            dst = xg.at[1, 0, pl.ds(i, 1), pl.ds(HEAD + HALF[d][0], 32)]
            k = 2 * (RC + i) + d
            z_second.append(start(remote(rz.at[d, pl.ds(i, 1)], dst, z_send.at[k], z_recv.at[k], who)))

    lane = lax.broadcasted_iota(jnp.int32, (S2, 128), 1)

    def compute(g):
        l, ux = g // 4, ORDER[g % 4]
        for r0, nr in ((0, 8), (8, 4)):
            late = xg[l, ux, r0:r0 + nr, HEAD:HEAD + WIN, :].reshape(nr * WIN, K)
            early = xg[l, ux, r0:r0 + nr, 0:WIN, :].reshape(nr * WIN, K)
            prod[:, r0 * WIN:(r0 + nr) * WIN] = lax.dot_general(
                op_all[...], jnp.concatenate([late, early], axis=1), (((1,), (1,)), ((), ())),
                preferred_element_type=jnp.float32)
        for j in range(NCH):
            acc = prod[0:S2, j * 4 * WIN:(j + 1) * 4 * WIN]
            for b in range(1, LAG // 2):
                acc = acc + pltpu.roll(prod[b * S2:(b + 1) * S2, j * 4 * WIN:(j + 1) * 4 * WIN], b, 1)
            v0, v1, v2 = acc[:, 0:128], acc[:, 128:256], acc[:, 256:384]
            index = g * NCH + j
            pairs = (jnp.where(lane < 64, v0, pltpu.roll(jnp.where(lane >= 96, v0, v1), 96, 1)),
                     jnp.where(lane < 64, pltpu.roll(v2, 96, 1), v1))
            for q in range(2):
                main[2 * index + q] = pairs[q]
                ex_out[2 * index + q] = pairs[q][8:24]
            halo = jnp.where(lane < 32, v2, jnp.where(lane < 64, v1, jnp.where(lane < 96, v0, v2)))
            half_f32[g * HR + j * S2:g * HR + (j + 1) * S2, :] = halo

    def halo_copy(g, k):
        return remote(halo_out.at[g], halo_in.at[k, g], halo_sem.at[16 * k + g], halo_sem.at[16 * k + 8 + g],
                      (after, cross_after)[k])

    def send_halo(g):
        halo_out[g] = half_f32[g * HR:(g + 1) * HR, :].astype(jnp.bfloat16)

        @pl.when(t < NTM - 1)
        def _():
            for k in range(2):
                halo_copy(g, k).start()

    lane8 = lax.broadcasted_iota(jnp.int32, (8, 128), 1)

    rows_of = [xs[d] * 48 for d in ORDER]

    def widen(g, j, q, first8, second8, base_s, core):
        for k in range(2):
            ry = 4 * j + ((0, 1), (3, 2))[q][k]
            row = rows_of[g % 4] + 24 * ((h + g // 4) % 2) + core * 3 + 6 * ys[ry // 3] + ry % 3
            mask = (lane8 < 64) if k == 0 else (lane8 >= 64)
            wide[pl.ds(base_s * STEP + row, 8, stride=STEP), :] = jnp.where(mask, second8, 0.0)
            wide[pl.ds(row, 8, stride=STEP), :] = jnp.where(mask, first8, 0.0)

    def exchange_copy(g):
        rows = pl.ds(g * 2 * NCH, 2 * NCH)
        return remote(ex_out.at[rows], ex_in.at[rows], ex_sem.at[g], ex_sem.at[8 + g], sibling)

    copies = {}

    def close(g):
        @pl.when(t > 0)
        def _():
            for k in range(2):
                halo_copy(g, k).wait_recv()

        copies[g].wait_recv()
        for k in range(2):
            halo = halo_in[k, g].astype(jnp.float32)
            for j in range(NCH):
                packed = halo[j * S2 + 8 * k:(j + 1) * S2]
                place = lane[8 * k:]
                by32, by64 = pltpu.roll(packed, 32, 1), pltpu.roll(packed, 64, 1)
                for q in range(2):
                    index = 2 * (g * NCH + j) + q
                    part = jnp.where(place < 64, by64, by32) if q == 0 else jnp.where(place < 64, by32, by64)
                    v = (main, ex_in)[k][index] + jnp.where(place % 64 < 32, part, 0.0)
                    if k == 0:
                        widen(g, j, q, v[0:8], v[16:24], 8, c)
                    else:
                        widen(g, j, q, v[0:8], v[8:16], 4, 1 - c)

    def unit(g):
        compute(g)
        send_halo(g)
        copies[g] = start(exchange_copy(g))

    round2(0)
    own_copy.wait()
    unit(0)
    round3(0)
    for n in (0, 1):
        for i in range(RC):
            z_second[2 * i + n].wait_recv()
        base(1, n)
    round4(0)
    unit(1)
    unit(2)
    round1(1)
    unit(3)
    close(0)
    close(1)
    round2(1)
    unit(4)
    close(2)
    flush(20)
    round3(1)
    close(3)
    flush(8)
    last(1, 1, 1)
    unit(5)
    last(1, 1, -1)
    unit(6)
    close(4)
    last(1, 1, 2)
    for oa in (-1, 1, 2):
        last(1, 0, oa)
    unit(7)
    for g in (5, 6, 7):
        close(g)

    both = lax.broadcasted_iota(jnp.int32, (TS, 128), 1) % TS == lax.broadcasted_iota(jnp.int32, (TS, 128), 0)
    both = jnp.where(both, 1.0, 0.0).astype(jnp.bfloat16)

    leaving = []
    for s in range(SH):
        block = wide[s * STEP:s * STEP + R, :].astype(jnp.bfloat16)
        result[s] = lax.dot_general(both, block, (((1,), (1,)), ((), ())),
                                    preferred_element_type=jnp.float32).astype(jnp.bfloat16)
        copy = pltpu.make_async_copy(result.at[s], out_ref.at[s], out_sem.at[s])
        copy.start()
        leaving.append(copy)

    flush(0)
    for copy in leaving:
        copy.wait()

    @pl.when(t < NTM - 1)
    def _():
        for g in range(8):
            for k in range(2):
                halo_copy(g, k).wait_send()


def body(shot_window, receiver_data, apertures, taper_index, taper_table):
    gathered = jnp.transpose(receiver_data, (1, 0, 2))
    bf, f4 = jnp.bfloat16, jnp.float32
    dma = pltpu.SemaphoreType.DMA
    out = pl.pallas_call(
        kernel,
        out_shape=jax.ShapeDtypeStruct((SH, TS, R), bf),
        in_specs=[pl.BlockSpec(memory_space=pltpu.HBM)] * 5,
        out_specs=pl.BlockSpec(memory_space=pl.ANY),
        scratch_shapes=[
            pltpu.VMEM((2, NX, UR, ROWS, K), bf),
            pltpu.VMEM((2, RC, 32, K), bf),
            pltpu.VMEM((4, SH), jnp.int32),
            pltpu.VMEM((4, SH), jnp.int32),
            pltpu.SMEM((16,), f4),
            pltpu.VMEM((SH, LAG, K), bf),
            pltpu.VMEM((SH, LAG, K), bf),
            pltpu.VMEM((SH, LAG, K), bf),
            pltpu.VMEM((2, LAG * S2, 128), f4),
            pltpu.VMEM((LAG * SH, 2 * K), bf),
            pltpu.VMEM((NKB, 128), f4),
            pltpu.VMEM((LAG * SH, UR * WIN), f4),
            pltpu.VMEM((48, S2, 128), f4),
            pltpu.VMEM((8 * HR, 128), f4),
            pltpu.VMEM((8, HR, 128), bf),
            pltpu.VMEM((2, 8, HR, 128), bf),
            pltpu.VMEM((48, 16, 128), f4),
            pltpu.VMEM((48, 16, 128), f4),
            pltpu.VMEM((16 * STEP, 128), f4),
            pltpu.VMEM((SH, TS, R), bf),
            dma((NSEM,)), dma((NSEM,)), dma((4 * RC,)), dma((4 * RC,)), dma((2,)), dma((32,)), dma((16,)), dma((SH,)), dma((5,)),
        ],
        compiler_params=pltpu.CompilerParams(collective_id=0, has_side_effects=True,
                                             vmem_limit_bytes=60 * 1024 * 1024),
    )(gathered, shot_window, apertures.T, taper_index.T, taper_table)
    return jnp.transpose(out, (1, 0, 2))


def solution(mesh):
    in_specs = (P("shot", None, None), P("tm", "shot", None), P("shot", None), P("shot", None), P())
    out_specs = P("tm", "shot", None)
    return jax.shard_map(body, mesh=mesh, in_specs=in_specs, out_specs=out_specs, check_vma=False)
```
